32 devices in a mesh: temporal: 4 (over z), spatial: 4 (over y, x), head: 2 (over core).
Axes of the slice: x: 2, y: 2, z: 4, core: 2. Of those that a mesh axis runs over, the one named last changes fastest.
Arguments:
- queries: bfloat16 [4096, 2048], P(('temporal', 'spatial'), 'head'), may hold values from -120 to 120
- keys: bfloat16 [4096, 2048], P(('temporal', 'spatial'), 'head'), may hold values from -6 to 6
- values: bfloat16 [4096, 2048], P(('temporal', 'spatial'), 'head'), may hold values from -6 to 6
- window: int32 [4, 1, 4, 27], P('temporal', None, 'spatial'), may hold values from 0 to 1, as said below
Outputs:
- attended: bfloat16 [4096, 2048], P(('temporal', 'spatial'), 'head')
The draws below stay inside these ranges and needn't reach their ends.
Inputs may be any that keep to these rules, and one draw needn't show every extreme that they name: `window`: entry 9 (dt + 1) + 3 (dh + 1) + (dw + 1) of a tile's pattern admits the key tile at offset (dt, dh, dw) in tiles along frames, rows and columns; entry 13 is 1 for every tile.
All inputs are finite; a program needn't handle non-finite values.
Results may differ from the reference program's by a relative error of at most 0.0028.
Values may be sent and summed in bfloat16 or wider, within the bound.
A program may use at most 64 MiB of HBM per device.

```python
import math
import jax
import jax.numpy as jnp
from jax import lax

D_HEAD = 128
HEADS = 16
TILE_T = 4
TILE_H = 8
TILE_W = 8
TH_TILES = 1
T_TILES = 4
W_TILES = 4
TOKENS = 4096
CHANNELS = 2048


def key_sample(key):
    folded = jax.random.fold_in(key, 7)
    first_key = jax.random.fold_in(folded, 0)
    extent = (TOKENS, HEADS * D_HEAD)
    sample = jax.random.normal(first_key, extent, jnp.float32)
    return jnp.clip(sample, -6.0, 6.0)


def draw_keys(key, part):
    return key_sample(key).astype(jnp.bfloat16)


def draw_queries(key, part):
    folded = jax.random.fold_in(key, 13)
    first_key = jax.random.fold_in(folded, 0)
    extent = (TOKENS, HEADS * D_HEAD)
    jitter = jax.random.normal(first_key, extent, jnp.float32)
    sample = 3.0 * jitter
    return jnp.clip(sample, -120.0, 120.0).astype(jnp.bfloat16)


def draw_window(key, part):
    folded = jax.random.fold_in(key, 3)
    levels = jax.random.randint(folded, (T_TILES, TH_TILES, W_TILES, 27), 0, 4)
    admitted = jnp.where(levels > 0, 1, 0).astype(jnp.int32)
    centre = jnp.arange(27, dtype=jnp.int32) == 13
    return jnp.where(centre[None, None, None, :], 1, admitted).astype(jnp.int32)


def block_scale(key, shape, cuts, smallest, largest):
    level = 1.0
    for position, blocks in cuts:
        heights = jax.random.uniform(jax.random.fold_in(jax.random.fold_in(key, 6), position), (blocks,), jnp.float32, smallest / len(cuts), largest / len(cuts))
        level = level * jnp.repeat(jnp.exp(heights), shape[position] // blocks).reshape((-1,) + (1,) * (len(shape) - 1 - position))
    return level


def scatter_about(own_key, shape, deviation, reach, shards=(), kind=jnp.bfloat16):
    values = deviation * jax.random.normal(own_key, shape, jnp.float32)
    if shards:
        values = values * block_scale(own_key, shape, shards, -0.22, 0.18)
    return jnp.clip(values, -reach, reach).astype(kind)


def setup_inputs(seed: int = 0) -> dict:
    seeds = jax.random.split(jax.random.key(seed), 5)
    queries = draw_queries(jax.random.fold_in(seeds[4], 71), 0)
    keys = draw_keys(jax.random.fold_in(seeds[4], 71), 0)
    values = scatter_about(seeds[2], (TOKENS, CHANNELS), 1.0, 6.0, ((0, 16), (1, 2)))
    window = draw_window(jax.random.fold_in(seeds[4], 71), 0)
    return dict(queries=queries, keys=keys, values=values, window=window)


def tile_mask(pattern, tile_row, first_row, window_rows, time_ok, width_ok):
    picked = []
    for offset in range(window_rows):
        height_step = first_row + offset - tile_row
        if -1 <= height_step <= 1:
            picked.append(pattern[:, height_step + 1, :] == 1)
        else:
            picked.append(jnp.zeros_like(pattern[:, 0, :]) == 1)
    chosen = jnp.stack(picked, axis=1)
    allowed = chosen & time_ok[:, None, None] & width_ok[None, None, :]
    return jnp.broadcast_to(allowed[:, None, :, None, :, None], (3, TILE_T, window_rows, TILE_H, 3, TILE_W)).reshape(-1)

def attend_all(query_tile, key_window, value_window, key_ok):
    scale = 1.0 / math.sqrt(D_HEAD)
    scores = jnp.einsum('qhd,khd->hqk', query_tile.astype(jnp.float32), key_window.astype(jnp.float32)) * scale
    scores = jnp.where(key_ok[None, None, :], scores, -jnp.inf)
    peak = lax.optimization_barrier(jnp.max(scores, axis=-1, keepdims=True))
    weights = jnp.exp(scores - peak)
    total = lax.optimization_barrier(jnp.sum(weights, axis=-1))
    rounded = lax.optimization_barrier(weights.astype(jnp.bfloat16))
    mixed = jnp.einsum('hqk,khd->qhd', rounded.astype(jnp.float32), value_window.astype(jnp.float32))
    mixed = mixed / jnp.transpose(total)[:, :, None]
    return mixed.astype(jnp.bfloat16).reshape(mixed.shape[0], -1)

def reference(queries, keys, values, window):
    channels = HEADS * D_HEAD
    tile_size = TILE_T * TILE_H * TILE_W
    shape_tiles = (T_TILES, TILE_T, TH_TILES, TILE_H, W_TILES, TILE_W, channels)
    query_tiles = queries.reshape(shape_tiles)
    padding = ((1, 1), (0, 0), (0, 0), (0, 0), (1, 1), (0, 0), (0, 0))
    key_padded = jnp.pad(keys.reshape(shape_tiles), padding)
    value_padded = jnp.pad(values.reshape(shape_tiles), padding)
    window_rows = min(3, TH_TILES)
    offsets = jnp.arange(3, dtype=jnp.int32) - 1
    results = []
    for tile_row in range(TH_TILES):
        first_row = min(max(tile_row - 1, 0), TH_TILES - window_rows)

        def one_tile(flat_index):
            time_tile = flat_index // W_TILES
            width_tile = flat_index % W_TILES
            zero = jnp.zeros((), jnp.int32)
            query_tile = lax.dynamic_slice(query_tiles, (time_tile, zero, zero + tile_row, zero, width_tile, zero, zero), (1, TILE_T, 1, TILE_H, 1, TILE_W, channels)).reshape(tile_size, HEADS, D_HEAD)
            corner = (time_tile, zero, zero + first_row, zero, width_tile, zero, zero)
            extent = (3, TILE_T, window_rows, TILE_H, 3, TILE_W, channels)
            key_window = lax.dynamic_slice(key_padded, corner, extent).reshape(-1, HEADS, D_HEAD)
            value_window = lax.dynamic_slice(value_padded, corner, extent).reshape(-1, HEADS, D_HEAD)
            pattern = lax.dynamic_slice(window, (time_tile, zero + tile_row, width_tile, zero), (1, 1, 1, 27)).reshape(3, 3, 3)
            time_index = time_tile + offsets
            width_index = width_tile + offsets
            time_ok = (time_index >= 0) & (time_index < T_TILES)
            width_ok = (width_index >= 0) & (width_index < W_TILES)
            key_ok = tile_mask(pattern, tile_row, first_row, window_rows, time_ok, width_ok)
            return attend_all(query_tile, key_window, value_window, key_ok)
        flat = lax.map(one_tile, jnp.arange(T_TILES * W_TILES, dtype=jnp.int32))
        results.append(flat.reshape(T_TILES, W_TILES, TILE_T, TILE_H, TILE_W, channels))
    stacked = jnp.stack(results, axis=2)
    ordered = jnp.transpose(stacked, (0, 3, 2, 4, 1, 5, 6))
    return ordered.reshape(TOKENS, channels)
```

```python
import functools
import math

import jax
import jax.numpy as jnp
from jax import lax
from jax.experimental import pallas as pl
from jax.experimental.pallas import tpu as pltpu
from jax.sharding import PartitionSpec as P

D_HEAD = 128
TILE_T = 4
TILE_H = 8
TILE_W = 8
MESH = pl.DeviceIdType.MESH


def with_halo(array, sides, width):
    for axis, dim in sides:
        peers, length = (lax.axis_size(axis), array.shape[dim])
        up = [(i, (i + 1) % peers) for i in range(peers - 1)]
        down = [(j, i) for i, j in up]
        last = lax.slice_in_dim(array, length - width, length, axis=dim)
        initial = lax.slice_in_dim(array, 0, width, axis=dim)
        before = lax.ppermute(last, axis, up)
        after = lax.ppermute(initial, axis, down)
        array = jnp.concatenate([before, array, after], axis=dim)
    return array


def tile_mask(pattern, tile_row, first_row, window_rows, time_ok, width_ok):
    height_step = first_row - tile_row
    picked = [pattern[:, height_step + 1, :] == 1]
    chosen = jnp.stack(picked, axis=1)
    allowed = chosen & time_ok[:, None, None] & width_ok[None, None, :]
    return jnp.broadcast_to(
        allowed[:, None, :, None, :, None], (3, TILE_T, window_rows, TILE_H, 3, TILE_W)
    ).reshape(-1)


def attend(query_tile, key_window, value_window, key_ok):
    heads_here = query_tile.shape[1]
    group = min(2, heads_here)
    scale = 1.0 / math.sqrt(D_HEAD)
    pieces = []
    for head_start in range(0, heads_here, group):
        query_part = query_tile[:, head_start : head_start + group]
        key_part = key_window[:, head_start : head_start + group]
        value_part = value_window[:, head_start : head_start + group]
        scores = (
            jnp.einsum("qhd,khd->hqk", query_part, key_part, preferred_element_type=jnp.float32)
            * scale
        )
        scores = jnp.where(key_ok[None, None, :], scores, -jnp.inf)
        peak = jnp.max(scores, axis=-1, keepdims=True)
        weights = jnp.exp(scores - peak)
        total = jnp.sum(weights, axis=-1)
        attended_part = jnp.einsum(
            "hqk,khd->qhd",
            weights.astype(jnp.bfloat16),
            value_part,
            preferred_element_type=jnp.float32,
        )
        attended_part = attended_part / jnp.transpose(total)[:, :, None]
        pieces.append(attended_part.astype(jnp.bfloat16).reshape(attended_part.shape[0], -1))
    return jnp.concatenate(pieces, axis=1)


def gathered(queries, keys, values, window):
    space_count = lax.axis_size("spatial")
    time_count = lax.axis_size("temporal")
    tokens_dev, channels = queries.shape
    tile_rows = window.shape[1]
    height = tile_rows * TILE_H
    shard_rows = tokens_dev // (space_count * TILE_W)
    split = 1
    groups = space_count // split
    span = split * TILE_W
    part_channels = channels // split

    def to_blocks(tensor):
        shaped = tensor.reshape(shard_rows, groups, span, split, part_channels)
        return jnp.transpose(shaped, (3, 1, 0, 2, 4)).reshape(
            space_count, shard_rows, span, part_channels
        )

    def from_blocks(tensor):
        return tensor.reshape(TILE_T, height, span, part_channels)

    query_block, key_block, value_block = (
        lax.all_to_all(to_blocks(queries), "spatial", split_axis=0, concat_axis=0, tiled=True),
        lax.all_to_all(to_blocks(keys), "spatial", split_axis=0, concat_axis=0, tiled=True),
        lax.all_to_all(to_blocks(values), "spatial", split_axis=0, concat_axis=0, tiled=True),
    )
    add_key_block = from_blocks(key_block)
    add_value_block = from_blocks(value_block)
    paired = jnp.stack([add_key_block, add_value_block]).reshape(
        2, 1, TILE_T, height, split, TILE_W, part_channels
    )
    padded = with_halo(paired, (("temporal", 1), ("spatial", 4)), 1)
    query_block = from_blocks(query_block)
    column_base = lax.axis_index("spatial")
    offsets = jnp.arange(3, dtype=jnp.int32) - 1
    time_index = lax.axis_index("temporal") + offsets
    time_ok = (time_index >= 0) & (time_index < time_count)
    window_rows = min(3, tile_rows)
    heads_here = part_channels // D_HEAD
    width_index = column_base + 0 + offsets
    width_ok = (width_index >= 0) & (width_index < space_count)
    pattern_column = lax.dynamic_index_in_dim(window, 0, 2, keepdims=False)
    pattern_rows = pattern_column.reshape(tile_rows, 3, 3, 3)
    first_row = min(max(0 - 1, 0), tile_rows - window_rows)
    key_ok = tile_mask(pattern_rows[0], 0, first_row, window_rows, time_ok, width_ok)
    query_tile = query_block.reshape(-1, heads_here, D_HEAD)
    row_low = first_row * TILE_H
    row_high = row_low + window_rows * TILE_H
    key_window = padded[0, :, :, row_low:row_high, 0:3].reshape(-1, heads_here, D_HEAD)
    value_window = padded[1, :, :, row_low:row_high, 0:3].reshape(-1, heads_here, D_HEAD)
    attended_tile = attend(query_tile, key_window, value_window, key_ok)
    outputs = attended_tile.reshape(TILE_T, TILE_H, TILE_W, part_channels)
    result = outputs.reshape(space_count, shard_rows, span, part_channels)
    returned = lax.all_to_all(result, "spatial", split_axis=0, concat_axis=0, tiled=True)
    shaped = returned.reshape(split, groups, shard_rows, span, part_channels)
    return jnp.transpose(shaped, (2, 1, 3, 0, 4)).reshape(tokens_dev, channels)


def flipped(index, bits):
    bit = 1
    while bit <= bits:
        if bits & bit:
            index = index + bit - 2 * bit * ((index // bit) % 2)
        bit *= 2
    return index


def by_tiles(rows, count):
    width = count * TILE_W
    whole = rows.astype(jnp.float32)
    lines = whole.shape[0] // width
    return [
        jnp.concatenate(
            [whole[r * width + w * TILE_W : r * width + (w + 1) * TILE_W] for r in range(lines)],
            axis=0,
        ).astype(rows.dtype)
        for w in range(count)
    ]


def by_rows(parts):
    parts = [part.astype(jnp.float32) for part in parts]
    lines = parts[0].shape[0] // TILE_W
    return jnp.concatenate(
        [part[r * TILE_W : (r + 1) * TILE_W] for r in range(lines) for part in parts], axis=0
    ).astype(jnp.bfloat16)


def fused_kernel(
    times, count, own_heads,
    q_ref, k_ref, v_ref, win_ref, out_ref,
    stage_kv, stage_q, kv, qs, outs, arrived, win,
    kv_send, kv_recv, q_send, q_recv, z_send, z_recv, o_send, o_recv, w_send, w_recv,
):
    t = lax.axis_index("temporal")
    me = lax.axis_index("spatial")
    part = q_ref.shape[0] // count
    peers = range(1, count)
    peer = [flipped(me, d) for d in range(count)]

    def rows_of(index):
        return pl.ds(pl.multiple_of(index * part, part), part)

    def columns_of(index, h):
        return pl.ds(pl.multiple_of((index * own_heads + h) * D_HEAD, D_HEAD), D_HEAD)

    def to(d):
        return {"spatial": peer[d]}

    def kv_copy(d, h, rows):
        return pltpu.make_async_remote_copy(
            src_ref=stage_kv.at[d - 1, h],
            dst_ref=kv.at[1, h, :, :, rows],
            send_sem=kv_send.at[d - 1, h],
            recv_sem=kv_recv.at[d - 1, h],
            device_id=to(d), device_id_type=MESH,
        )

    def q_copy(d, h, rows):
        return pltpu.make_async_remote_copy(
            src_ref=stage_q.at[d - 1, h],
            dst_ref=qs.at[h, :, rows],
            send_sem=q_send.at[d - 1, h],
            recv_sem=q_recv.at[d - 1, h],
            device_id=to(d), device_id_type=MESH,
        )

    def w_copy(d, slot):
        return pltpu.make_async_remote_copy(
            src_ref=win.at[slot],
            dst_ref=win.at[slot],
            send_sem=w_send.at[d - 1],
            recv_sem=w_recv.at[d - 1],
            device_id=to(d), device_id_type=MESH,
        )

    def z_copy(side, d, h):
        rows = rows_of(peer[d])
        return pltpu.make_async_remote_copy(
            src_ref=kv.at[1, h, :, :, rows],
            dst_ref=kv.at[2 * side, h, :, :, rows],
            send_sem=z_send.at[side, d, h],
            recv_sem=z_recv.at[side, d, h],
            device_id={"temporal": t + 1 - 2 * side}, device_id_type=MESH,
        )

    def o_copy(d, h, w):
        return pltpu.make_async_remote_copy(
            src_ref=outs.at[h, w, rows_of(peer[d])],
            dst_ref=arrived.at[d - 1, h, w],
            send_sem=o_send.at[d - 1, h, w],
            recv_sem=o_recv.at[d - 1, h, w],
            device_id=to(d), device_id_type=MESH,
        )

    can_send = (t < times - 1, t > 0)
    can_take = (t > 0, t < times - 1)

    barrier = pltpu.get_barrier_semaphore()
    for d in peers:
        pl.semaphore_signal(barrier, inc=1, device_id=to(d), device_id_type=MESH)
    for side in range(2):
        @pl.when(can_send[side])
        def _(side=side):
            pl.semaphore_signal(
                barrier, inc=1, device_id={"temporal": t + 1 - 2 * side}, device_id_type=MESH
            )

    def lay_kv(d, h):
        for i, ref in enumerate((k_ref, v_ref)):
            for w, piece in enumerate(by_tiles(ref[:, columns_of(peer[d], h)], count)):
                if d:
                    stage_kv[d - 1, h, i, w] = piece
                else:
                    kv[1, h, i, w, rows_of(me)] = piece

    def lay_q(d, h):
        for w, piece in enumerate(by_tiles(q_ref[:, columns_of(peer[d], h)], count)):
            if d:
                stage_q[d - 1, h, w] = piece
            else:
                qs[h, w, rows_of(me)] = piece

    def forward(d, h):
        for side in range(2):
            @pl.when(can_send[side])
            def _(side=side):
                z_copy(side, d, h).start()

    lay_kv(0, 0)
    win[me] = jnp.zeros(win.shape[1:], win.dtype)
    win[me, 0:1, 0 : win_ref.shape[1]] = win_ref[...]
    for side in range(2):
        @pl.when(jnp.logical_not(can_take[side]))
        def _(side=side):
            kv[2 * side] = jnp.zeros(kv.shape[1:], kv.dtype)

    linked = can_send[0].astype(jnp.int32) + can_send[1].astype(jnp.int32)
    pl.semaphore_wait(barrier, count - 1 + linked)

    for h in range(own_heads):
        if h:
            lay_kv(0, h)
        forward(0, h)
        for d in peers:
            lay_kv(d, h)
            kv_copy(d, h, rows_of(me)).start()
    for d in peers:
        w_copy(d, me).start()
    for h in range(own_heads):
        for d in peers:
            lay_q(d, h)
            q_copy(d, h, rows_of(me)).start()
        lay_q(0, h)

    for h in range(own_heads):
        for d in peers:
            kv_copy(d, h, rows_of(peer[d])).wait_recv()
            forward(d, h)
    for d in peers:
        w_copy(d, peer[d]).wait_recv()

    factor = math.log2(math.e) / math.sqrt(D_HEAD)
    for h in range(own_heads):
        for d in peers:
            q_copy(d, h, rows_of(peer[d])).wait_recv()
        for side in range(2):
            @pl.when(can_take[side])
            def _(side=side):
                for d in range(count):
                    z_copy(side, d, h).wait_recv()
        for w in range(count):
            low, high = max(w - 1, 0), min(w + 2, count)
            query = qs[h, w]
            pattern = win[w, 0:1, :]
            scores, limits = [], []
            for p in range(3):
                for c in range(low, high):
                    scores.append(lax.dot_general(
                        query, kv[p, h, 0, c], (((1,), (1,)), ((), ())),
                        preferred_element_type=jnp.float32,
                    ))
                    entry = 9 * p + 3 + (c - w + 1)
                    ok = pattern[:, entry : entry + 1] == 1
                    if p != 1:
                        ok = jnp.logical_and(ok, can_take[p // 2])
                    limits.append(jnp.where(ok, 0.0, jnp.inf).astype(jnp.float32))
            peak = None
            for score, limit in zip(scores, limits):
                top = jnp.max(score, axis=1, keepdims=True) - limit
                peak = top if peak is None else jnp.maximum(peak, top)
            total, mixed = None, None
            for i, (score, limit) in enumerate(zip(scores, limits)):
                p, c = i // (high - low), low + i % (high - low)
                weights = jnp.exp2((score - (peak + limit)) * factor)
                part_total = jnp.sum(weights, axis=1, keepdims=True)
                part_mixed = jnp.dot(
                    weights.astype(jnp.bfloat16), kv[p, h, 1, c],
                    preferred_element_type=jnp.float32,
                )
                total = part_total if total is None else total + part_total
                mixed = part_mixed if mixed is None else mixed + part_mixed
            outs[h, w] = (mixed / total).astype(jnp.bfloat16)
            for d in peers:
                o_copy(d, h, w).start()

    for h in range(own_heads):
        out_ref[:, columns_of(me, h)] = by_rows([outs[h, w, rows_of(me)] for w in range(count)])
        for d in peers:
            for w in range(count):
                o_copy(d, h, w).wait_recv()
            out_ref[:, columns_of(peer[d], h)] = by_rows([arrived[d - 1, h, w] for w in range(count)])

    for h in range(own_heads):
        for d in peers:
            kv_copy(d, h, rows_of(me)).wait_send()
            q_copy(d, h, rows_of(me)).wait_send()
            for w in range(count):
                o_copy(d, h, w).wait_send()
        for side in range(2):
            @pl.when(can_send[side])
            def _(side=side):
                for d in range(count):
                    z_copy(side, d, h).wait_send()
    for d in peers:
        w_copy(d, me).wait_send()


def fused(queries, keys, values, window):
    count, times = lax.axis_size("spatial"), lax.axis_size("temporal")
    tokens, channels = queries.shape
    own = channels // (D_HEAD * count)
    part = tokens // count
    vmem = pl.BlockSpec(memory_space=pltpu.VMEM)
    dma = pltpu.SemaphoreType.DMA
    pairs = own * count * (3 * count - 2) * 3 * tokens * tokens * D_HEAD
    return pl.pallas_call(
        functools.partial(fused_kernel, times, count, own),
        out_shape=jax.ShapeDtypeStruct(queries.shape, queries.dtype),
        in_specs=[vmem] * 4,
        out_specs=vmem,
        scratch_shapes=[
            pltpu.VMEM((count - 1, own, 2, count, part, D_HEAD), jnp.bfloat16),
            pltpu.VMEM((count - 1, own, count, part, D_HEAD), jnp.bfloat16),
            pltpu.VMEM((3, own, 2, count, tokens, D_HEAD), jnp.bfloat16),
            pltpu.VMEM((own, count, tokens, D_HEAD), jnp.bfloat16),
            pltpu.VMEM((own, count, tokens, D_HEAD), jnp.bfloat16),
            pltpu.VMEM((count - 1, own, count, part, D_HEAD), jnp.bfloat16),
            pltpu.VMEM((count, 8, 128), jnp.int32),
            dma((count - 1, own)), dma((count - 1, own)),
            dma((count - 1, own)), dma((count - 1, own)),
            dma((2, count, own)), dma((2, count, own)),
            dma((count - 1, own, count)), dma((count - 1, own, count)),
            dma((count - 1,)), dma((count - 1,)),
        ],
        compiler_params=pltpu.CompilerParams(
            collective_id=0, has_side_effects=True, vmem_limit_bytes=48 * 2**20
        ),
        cost_estimate=pl.CostEstimate(
            flops=4 * pairs, bytes_accessed=4 * tokens * channels * 2, transcendentals=pairs // D_HEAD
        ),
    )(queries, keys, values, window.reshape(1, -1))


def body(queries, keys, values, window):
    count = lax.axis_size("spatial")
    tokens, channels = queries.shape
    heads_here = channels // D_HEAD
    whole_tiles = window.shape[1] == 1 and window.shape[2] == 1 and tokens == TILE_T * TILE_H * TILE_W
    if whole_tiles and count & (count - 1) == 0 and heads_here % count == 0:
        return fused(queries, keys, values, window)
    return gathered(queries, keys, values, window)


def solution(mesh):
    return jax.shard_map(
        body,
        mesh=mesh,
        in_specs=(
            P(("temporal", "spatial"), "head"),
            P(("temporal", "spatial"), "head"),
            P(("temporal", "spatial"), "head"),
            P("temporal", None, "spatial", None),
        ),
        out_specs=P(("temporal", "spatial"), "head"),
        check_vma=False,
    )
```

```python
import functools
import math

import jax
import jax.numpy as jnp
from jax import lax
from jax.experimental import pallas as pl
from jax.experimental.pallas import tpu as pltpu
from jax.sharding import PartitionSpec as P

D_HEAD = 128
TILE_T = 4
TILE_H = 8
TILE_W = 8
LANES = 128
MESH = pl.DeviceIdType.MESH


def with_halo(array, sides, width):
    for axis, dim in sides:
        peers, length = (lax.axis_size(axis), array.shape[dim])
        up = [(i, (i + 1) % peers) for i in range(peers - 1)]
        down = [(j, i) for i, j in up]
        last = lax.slice_in_dim(array, length - width, length, axis=dim)
        initial = lax.slice_in_dim(array, 0, width, axis=dim)
        before = lax.ppermute(last, axis, up)
        after = lax.ppermute(initial, axis, down)
        array = jnp.concatenate([before, array, after], axis=dim)
    return array


def tile_mask(pattern, tile_row, first_row, window_rows, time_ok, width_ok):
    height_step = first_row - tile_row
    picked = [pattern[:, height_step + 1, :] == 1]
    chosen = jnp.stack(picked, axis=1)
    allowed = chosen & time_ok[:, None, None] & width_ok[None, None, :]
    return jnp.broadcast_to(
        allowed[:, None, :, None, :, None], (3, TILE_T, window_rows, TILE_H, 3, TILE_W)
    ).reshape(-1)


def attend(query_tile, key_window, value_window, key_ok):
    heads_here = query_tile.shape[1]
    group = min(2, heads_here)
    scale = 1.0 / math.sqrt(D_HEAD)
    pieces = []
    for head_start in range(0, heads_here, group):
        query_part = query_tile[:, head_start : head_start + group]
        key_part = key_window[:, head_start : head_start + group]
        value_part = value_window[:, head_start : head_start + group]
        scores = (
            jnp.einsum("qhd,khd->hqk", query_part, key_part, preferred_element_type=jnp.float32)
            * scale
        )
        scores = jnp.where(key_ok[None, None, :], scores, -jnp.inf)
        peak = jnp.max(scores, axis=-1, keepdims=True)
        weights = jnp.exp(scores - peak)
        total = jnp.sum(weights, axis=-1)
        attended_part = jnp.einsum(
            "hqk,khd->qhd",
            weights.astype(jnp.bfloat16),
            value_part,
            preferred_element_type=jnp.float32,
        )
        attended_part = attended_part / jnp.transpose(total)[:, :, None]
        pieces.append(attended_part.astype(jnp.bfloat16).reshape(attended_part.shape[0], -1))
    return jnp.concatenate(pieces, axis=1)


def gathered(queries, keys, values, window):
    space_count = lax.axis_size("spatial")
    time_count = lax.axis_size("temporal")
    tokens_dev, channels = queries.shape
    tile_rows = window.shape[1]
    height = tile_rows * TILE_H
    shard_rows = tokens_dev // (space_count * TILE_W)
    split = 1
    groups = space_count // split
    span = split * TILE_W
    part_channels = channels // split

    def to_blocks(tensor):
        shaped = tensor.reshape(shard_rows, groups, span, split, part_channels)
        return jnp.transpose(shaped, (3, 1, 0, 2, 4)).reshape(
            space_count, shard_rows, span, part_channels
        )

    def from_blocks(tensor):
        return tensor.reshape(TILE_T, height, span, part_channels)

    query_block, key_block, value_block = (
        lax.all_to_all(to_blocks(queries), "spatial", split_axis=0, concat_axis=0, tiled=True),
        lax.all_to_all(to_blocks(keys), "spatial", split_axis=0, concat_axis=0, tiled=True),
        lax.all_to_all(to_blocks(values), "spatial", split_axis=0, concat_axis=0, tiled=True),
    )
    add_key_block = from_blocks(key_block)
    add_value_block = from_blocks(value_block)
    paired = jnp.stack([add_key_block, add_value_block]).reshape(
        2, 1, TILE_T, height, split, TILE_W, part_channels
    )
    padded = with_halo(paired, (("temporal", 1), ("spatial", 4)), 1)
    query_block = from_blocks(query_block)
    column_base = lax.axis_index("spatial")
    offsets = jnp.arange(3, dtype=jnp.int32) - 1
    time_index = lax.axis_index("temporal") + offsets
    time_ok = (time_index >= 0) & (time_index < time_count)
    window_rows = min(3, tile_rows)
    heads_here = part_channels // D_HEAD
    width_index = column_base + 0 + offsets
    width_ok = (width_index >= 0) & (width_index < space_count)
    pattern_column = lax.dynamic_index_in_dim(window, 0, 2, keepdims=False)
    pattern_rows = pattern_column.reshape(tile_rows, 3, 3, 3)
    first_row = min(max(0 - 1, 0), tile_rows - window_rows)
    key_ok = tile_mask(pattern_rows[0], 0, first_row, window_rows, time_ok, width_ok)
    query_tile = query_block.reshape(-1, heads_here, D_HEAD)
    row_low = first_row * TILE_H
    row_high = row_low + window_rows * TILE_H
    key_window = padded[0, :, :, row_low:row_high, 0:3].reshape(-1, heads_here, D_HEAD)
    value_window = padded[1, :, :, row_low:row_high, 0:3].reshape(-1, heads_here, D_HEAD)
    attended_tile = attend(query_tile, key_window, value_window, key_ok)
    outputs = attended_tile.reshape(TILE_T, TILE_H, TILE_W, part_channels)
    result = outputs.reshape(space_count, shard_rows, span, part_channels)
    returned = lax.all_to_all(result, "spatial", split_axis=0, concat_axis=0, tiled=True)
    shaped = returned.reshape(split, groups, shard_rows, span, part_channels)
    return jnp.transpose(shaped, (2, 1, 3, 0, 4)).reshape(tokens_dev, channels)


def flipped(index, bits):
    bit = 1
    while bit <= bits:
        if bits & bit:
            index = index + bit - 2 * bit * ((index // bit) % 2)
        bit *= 2
    return index


def by_tiles(rows, count):
    width = count * TILE_W
    whole = rows.astype(jnp.float32)
    lines = whole.shape[0] // width
    return [
        jnp.concatenate(
            [whole[r * width + w * TILE_W : r * width + (w + 1) * TILE_W] for r in range(lines)],
            axis=0,
        ).astype(rows.dtype)
        for w in range(count)
    ]


def by_rows(parts):
    parts = [part.astype(jnp.float32) for part in parts]
    lines = parts[0].shape[0] // TILE_W
    return jnp.concatenate(
        [part[r * TILE_W : (r + 1) * TILE_W] for r in range(lines) for part in parts], axis=0
    ).astype(jnp.bfloat16)


def fused_kernel(
    times, count, own_heads,
    q_hbm, k_hbm, v_hbm, win_hbm, out_ref,
    q_ref, k_ref, v_ref, win_ref, stage_kv, stage_q, kv, qs, outs, arrived, win,
    kv_send, kv_recv, q_send, q_recv, z_send, z_recv, o_send, o_recv, w_send, w_recv,
    in_sem, win_sem,
):
    t = lax.axis_index("temporal")
    me = lax.axis_index("spatial")
    part = q_ref.shape[0] // count
    peers = range(1, count)
    peer = [flipped(me, d) for d in range(count)]

    def rows_of(index):
        return pl.ds(pl.multiple_of(index * part, part), part)

    def columns_of(index, h):
        return pl.ds(pl.multiple_of((index * own_heads + h) * D_HEAD, D_HEAD), D_HEAD)

    def to(d):
        return {"spatial": peer[d]}

    def kv_copy(d, h, rows):
        return pltpu.make_async_remote_copy(
            src_ref=stage_kv.at[d - 1, h],
            dst_ref=kv.at[1, h, :, :, rows],
            send_sem=kv_send.at[d - 1, h],
            recv_sem=kv_recv.at[d - 1, h],
            device_id=to(d), device_id_type=MESH,
        )

    def q_copy(d, h, rows):
        return pltpu.make_async_remote_copy(
            src_ref=stage_q.at[d - 1, h],
            dst_ref=qs.at[h, :, rows],
            send_sem=q_send.at[d - 1, h],
            recv_sem=q_recv.at[d - 1, h],
            device_id=to(d), device_id_type=MESH,
        )

    def w_copy(d, slot):
        return pltpu.make_async_remote_copy(
            src_ref=win.at[slot],
            dst_ref=win.at[slot],
            send_sem=w_send.at[d - 1],
            recv_sem=w_recv.at[d - 1],
            device_id=to(d), device_id_type=MESH,
        )

    def z_copy(side, d, h):
        rows = rows_of(peer[d])
        return pltpu.make_async_remote_copy(
            src_ref=kv.at[1, h, :, :, rows],
            dst_ref=kv.at[2 * side, h, :, :, rows],
            send_sem=z_send.at[side, d, h],
            recv_sem=z_recv.at[side, d, h],
            device_id={"temporal": t + 1 - 2 * side}, device_id_type=MESH,
        )

    def o_copy(d, h, w):
        return pltpu.make_async_remote_copy(
            src_ref=outs.at[h, w, rows_of(peer[d])],
            dst_ref=arrived.at[d - 1, h, w],
            send_sem=o_send.at[d - 1, h, w],
            recv_sem=o_recv.at[d - 1, h, w],
            device_id=to(d), device_id_type=MESH,
        )

    def in_copy(i, d, h):
        here = columns_of(peer[d], h)
        return pltpu.make_async_copy(
            (k_hbm, v_hbm, q_hbm)[i].at[:, here],
            (k_ref, v_ref, q_ref)[i].at[:, here],
            in_sem.at[i, d, h],
        )

    for h in range(own_heads):
        for d in range(count):
            for i in range(2):
                in_copy(i, d, h).start()
    win_copy = pltpu.make_async_copy(win_hbm, win_ref, win_sem)
    win_copy.start()
    for h in range(own_heads):
        for d in range(count):
            in_copy(2, d, h).start()

    can_send = (t < times - 1, t > 0)
    can_take = (t > 0, t < times - 1)

    barrier = pltpu.get_barrier_semaphore()
    for d in peers:
        pl.semaphore_signal(barrier, inc=1, device_id=to(d), device_id_type=MESH)
    for side in range(2):
        @pl.when(can_send[side])
        def _(side=side):
            pl.semaphore_signal(
                barrier, inc=1, device_id={"temporal": t + 1 - 2 * side}, device_id_type=MESH
            )

    def lay_kv(d, h):
        for i, ref in enumerate((k_ref, v_ref)):
            in_copy(i, d, h).wait()
            for w, piece in enumerate(by_tiles(ref[:, columns_of(peer[d], h)], count)):
                if d:
                    stage_kv[d - 1, h, i, w] = piece
                else:
                    kv[1, h, i, w, rows_of(me)] = piece

    def lay_q(d, h):
        in_copy(2, d, h).wait()
        for w, piece in enumerate(by_tiles(q_ref[:, columns_of(peer[d], h)], count)):
            if d:
                stage_q[d - 1, h, w] = piece
            else:
                qs[h, w, rows_of(me)] = piece

    def forward(d, h):
        for side in range(2):
            @pl.when(can_send[side])
            def _(side=side):
                z_copy(side, d, h).start()

    lay_kv(0, 0)
    win_copy.wait()
    win[me] = jnp.zeros(win.shape[1:], win.dtype)
    win[me, 0:1, 0 : win_ref.shape[1]] = win_ref[...]
    for side in range(2):
        @pl.when(jnp.logical_not(can_take[side]))
        def _(side=side):
            kv[2 * side] = jnp.zeros(kv.shape[1:], kv.dtype)

    linked = can_send[0].astype(jnp.int32) + can_send[1].astype(jnp.int32)
    pl.semaphore_wait(barrier, count - 1 + linked)

    for h in range(own_heads):
        if h:
            lay_kv(0, h)
        forward(0, h)
        for d in peers:
            lay_kv(d, h)
            kv_copy(d, h, rows_of(me)).start()
    for d in peers:
        w_copy(d, me).start()
    for h in range(own_heads):
        for d in peers:
            lay_q(d, h)
            q_copy(d, h, rows_of(me)).start()
        lay_q(0, h)

    for h in range(own_heads):
        for d in peers:
            kv_copy(d, h, rows_of(peer[d])).wait_recv()
            forward(d, h)
    for d in peers:
        w_copy(d, peer[d]).wait_recv()

    factor = math.log2(math.e) / math.sqrt(D_HEAD)
    for h in range(own_heads):
        for d in peers:
            q_copy(d, h, rows_of(peer[d])).wait_recv()
        for side in range(2):
            @pl.when(can_take[side])
            def _(side=side):
                for d in range(count):
                    z_copy(side, d, h).wait_recv()
        for w in range(count):
            low, high = max(w - 1, 0), min(w + 2, count)
            query = qs[h, w]
            pattern = win[w, 0:1, :]
            wide = high - low
            keys = kv[:, h, 0, low:high].reshape(-1, D_HEAD)
            scores = lax.dot_general(
                query, keys, (((1,), (1,)), ((), ())), preferred_element_type=jnp.float32
            )
            blocks, limits, peak = [], [], None
            for i in range(3 * wide):
                p, c = i // wide, low + i % wide
                start = i * query.shape[0]
                halves = [
                    scores[:, j : j + LANES] for j in range(start, start + query.shape[0], LANES)
                ]
                entry = 9 * p + 3 + (c - w + 1)
                ok = pattern[:, entry : entry + 1] == 1
                if p != 1:
                    ok = jnp.logical_and(ok, can_take[p // 2])
                limit = jnp.where(ok, 0.0, jnp.inf).astype(jnp.float32)
                top = functools.reduce(jnp.maximum, halves) - limit
                peak = top if peak is None else jnp.maximum(peak, top)
                blocks.append(halves)
                limits.append(limit)
            peak = jnp.broadcast_to(jnp.max(peak, axis=1, keepdims=True), peak.shape)
            total, rounded = None, []
            for halves, limit in zip(blocks, limits):
                base = peak + limit
                for half in halves:
                    weights = jnp.exp2((half - base) * factor)
                    total = weights if total is None else total + weights
                    rounded.append(weights.astype(jnp.bfloat16))
            total = jnp.sum(total, axis=1, keepdims=True)
            mixed = jnp.dot(
                jnp.concatenate(rounded, axis=1),
                kv[:, h, 1, low:high].reshape(-1, D_HEAD),
                preferred_element_type=jnp.float32,
            )
            outs[h, w] = (mixed / total).astype(jnp.bfloat16)
            for d in peers:
                o_copy(d, h, w).start()

    for h in range(own_heads):
        out_ref[:, columns_of(me, h)] = by_rows([outs[h, w, rows_of(me)] for w in range(count)])
        for d in peers:
            for w in range(count):
                o_copy(d, h, w).wait_recv()
            out_ref[:, columns_of(peer[d], h)] = by_rows([arrived[d - 1, h, w] for w in range(count)])

    for h in range(own_heads):
        for d in peers:
            kv_copy(d, h, rows_of(me)).wait_send()
            q_copy(d, h, rows_of(me)).wait_send()
            for w in range(count):
                o_copy(d, h, w).wait_send()
        for side in range(2):
            @pl.when(can_send[side])
            def _(side=side):
                for d in range(count):
                    z_copy(side, d, h).wait_send()
    for d in peers:
        w_copy(d, me).wait_send()


def fused(queries, keys, values, window):
    count, times = lax.axis_size("spatial"), lax.axis_size("temporal")
    tokens, channels = queries.shape
    own = channels // (D_HEAD * count)
    part = tokens // count
    vmem = pl.BlockSpec(memory_space=pltpu.VMEM)
    dma = pltpu.SemaphoreType.DMA
    pairs = own * count * (3 * count - 2) * 3 * tokens * tokens * D_HEAD
    return pl.pallas_call(
        functools.partial(fused_kernel, times, count, own),
        out_shape=jax.ShapeDtypeStruct(queries.shape, queries.dtype),
        in_specs=[pl.BlockSpec(memory_space=pl.ANY)] * 4,
        out_specs=vmem,
        scratch_shapes=[
            pltpu.VMEM(queries.shape, jnp.bfloat16),
            pltpu.VMEM(queries.shape, jnp.bfloat16),
            pltpu.VMEM(queries.shape, jnp.bfloat16),
            pltpu.VMEM((1, window.size), jnp.int32),
            pltpu.VMEM((count - 1, own, 2, count, part, D_HEAD), jnp.bfloat16),
            pltpu.VMEM((count - 1, own, count, part, D_HEAD), jnp.bfloat16),
            pltpu.VMEM((3, own, 2, count, tokens, D_HEAD), jnp.bfloat16),
            pltpu.VMEM((own, count, tokens, D_HEAD), jnp.bfloat16),
            pltpu.VMEM((own, count, tokens, D_HEAD), jnp.bfloat16),
            pltpu.VMEM((count - 1, own, count, part, D_HEAD), jnp.bfloat16),
            pltpu.VMEM((count, 8, 128), jnp.int32),
            dma((count - 1, own)), dma((count - 1, own)),
            dma((count - 1, own)), dma((count - 1, own)),
            dma((2, count, own)), dma((2, count, own)),
            dma((count - 1, own, count)), dma((count - 1, own, count)),
            dma((count - 1,)), dma((count - 1,)),
            dma((3, count, own)), dma,
        ],
        compiler_params=pltpu.CompilerParams(
            collective_id=0, has_side_effects=True, vmem_limit_bytes=60 * 2**20
        ),
        cost_estimate=pl.CostEstimate(
            flops=4 * pairs, bytes_accessed=4 * tokens * channels * 2, transcendentals=pairs // D_HEAD
        ),
    )(queries, keys, values, window.reshape(1, -1))


def body(queries, keys, values, window):
    count = lax.axis_size("spatial")
    tokens, channels = queries.shape
    heads_here = channels // D_HEAD
    whole_tiles = window.shape[1] == 1 and window.shape[2] == 1 and tokens == TILE_T * TILE_H * TILE_W
    if whole_tiles and count & (count - 1) == 0 and heads_here % count == 0:
        return fused(queries, keys, values, window)
    return gathered(queries, keys, values, window)


def solution(mesh):
    return jax.shard_map(
        body,
        mesh=mesh,
        in_specs=(
            P(("temporal", "spatial"), "head"),
            P(("temporal", "spatial"), "head"),
            P(("temporal", "spatial"), "head"),
            P("temporal", None, "spatial", None),
        ),
        out_specs=P(("temporal", "spatial"), "head"),
        check_vma=False,
    )
```

```python
import functools
import math

import jax
import jax.numpy as jnp
from jax import lax
from jax.experimental import pallas as pl
from jax.experimental.pallas import tpu as pltpu
from jax.sharding import PartitionSpec as P

D_HEAD = 128
TILE_T = 4
TILE_H = 8
TILE_W = 8
LANES = 128
MESH = pl.DeviceIdType.MESH


def with_halo(array, sides, width):
    for axis, dim in sides:
        peers, length = (lax.axis_size(axis), array.shape[dim])
        up = [(i, (i + 1) % peers) for i in range(peers - 1)]
        down = [(j, i) for i, j in up]
        last = lax.slice_in_dim(array, length - width, length, axis=dim)
        initial = lax.slice_in_dim(array, 0, width, axis=dim)
        before = lax.ppermute(last, axis, up)
        after = lax.ppermute(initial, axis, down)
        array = jnp.concatenate([before, array, after], axis=dim)
    return array


def tile_mask(pattern, tile_row, first_row, window_rows, time_ok, width_ok):
    height_step = first_row - tile_row
    picked = [pattern[:, height_step + 1, :] == 1]
    chosen = jnp.stack(picked, axis=1)
    allowed = chosen & time_ok[:, None, None] & width_ok[None, None, :]
    return jnp.broadcast_to(
        allowed[:, None, :, None, :, None], (3, TILE_T, window_rows, TILE_H, 3, TILE_W)
    ).reshape(-1)


def attend(query_tile, key_window, value_window, key_ok):
    heads_here = query_tile.shape[1]
    group = min(2, heads_here)
    scale = 1.0 / math.sqrt(D_HEAD)
    pieces = []
    for head_start in range(0, heads_here, group):
        query_part = query_tile[:, head_start : head_start + group]
        key_part = key_window[:, head_start : head_start + group]
        value_part = value_window[:, head_start : head_start + group]
        scores = (
            jnp.einsum("qhd,khd->hqk", query_part, key_part, preferred_element_type=jnp.float32)
            * scale
        )
        scores = jnp.where(key_ok[None, None, :], scores, -jnp.inf)
        peak = jnp.max(scores, axis=-1, keepdims=True)
        weights = jnp.exp(scores - peak)
        total = jnp.sum(weights, axis=-1)
        attended_part = jnp.einsum(
            "hqk,khd->qhd",
            weights.astype(jnp.bfloat16),
            value_part,
            preferred_element_type=jnp.float32,
        )
        attended_part = attended_part / jnp.transpose(total)[:, :, None]
        pieces.append(attended_part.astype(jnp.bfloat16).reshape(attended_part.shape[0], -1))
    return jnp.concatenate(pieces, axis=1)


def gathered(queries, keys, values, window):
    space_count = lax.axis_size("spatial")
    time_count = lax.axis_size("temporal")
    tokens_dev, channels = queries.shape
    tile_rows = window.shape[1]
    height = tile_rows * TILE_H
    shard_rows = tokens_dev // (space_count * TILE_W)
    split = 1
    groups = space_count // split
    span = split * TILE_W
    part_channels = channels // split

    def to_blocks(tensor):
        shaped = tensor.reshape(shard_rows, groups, span, split, part_channels)
        return jnp.transpose(shaped, (3, 1, 0, 2, 4)).reshape(
            space_count, shard_rows, span, part_channels
        )

    def from_blocks(tensor):
        return tensor.reshape(TILE_T, height, span, part_channels)

    query_block, key_block, value_block = (
        lax.all_to_all(to_blocks(queries), "spatial", split_axis=0, concat_axis=0, tiled=True),
        lax.all_to_all(to_blocks(keys), "spatial", split_axis=0, concat_axis=0, tiled=True),
        lax.all_to_all(to_blocks(values), "spatial", split_axis=0, concat_axis=0, tiled=True),
    )
    add_key_block = from_blocks(key_block)
    add_value_block = from_blocks(value_block)
    paired = jnp.stack([add_key_block, add_value_block]).reshape(
        2, 1, TILE_T, height, split, TILE_W, part_channels
    )
    padded = with_halo(paired, (("temporal", 1), ("spatial", 4)), 1)
    query_block = from_blocks(query_block)
    column_base = lax.axis_index("spatial")
    offsets = jnp.arange(3, dtype=jnp.int32) - 1
    time_index = lax.axis_index("temporal") + offsets
    time_ok = (time_index >= 0) & (time_index < time_count)
    window_rows = min(3, tile_rows)
    heads_here = part_channels // D_HEAD
    width_index = column_base + 0 + offsets
    width_ok = (width_index >= 0) & (width_index < space_count)
    pattern_column = lax.dynamic_index_in_dim(window, 0, 2, keepdims=False)
    pattern_rows = pattern_column.reshape(tile_rows, 3, 3, 3)
    first_row = min(max(0 - 1, 0), tile_rows - window_rows)
    key_ok = tile_mask(pattern_rows[0], 0, first_row, window_rows, time_ok, width_ok)
    query_tile = query_block.reshape(-1, heads_here, D_HEAD)
    row_low = first_row * TILE_H
    row_high = row_low + window_rows * TILE_H
    key_window = padded[0, :, :, row_low:row_high, 0:3].reshape(-1, heads_here, D_HEAD)
    value_window = padded[1, :, :, row_low:row_high, 0:3].reshape(-1, heads_here, D_HEAD)
    attended_tile = attend(query_tile, key_window, value_window, key_ok)
    outputs = attended_tile.reshape(TILE_T, TILE_H, TILE_W, part_channels)
    result = outputs.reshape(space_count, shard_rows, span, part_channels)
    returned = lax.all_to_all(result, "spatial", split_axis=0, concat_axis=0, tiled=True)
    shaped = returned.reshape(split, groups, shard_rows, span, part_channels)
    return jnp.transpose(shaped, (2, 1, 3, 0, 4)).reshape(tokens_dev, channels)


def flipped(index, bits):
    bit = 1
    while bit <= bits:
        if bits & bit:
            index = index + bit - 2 * bit * ((index // bit) % 2)
        bit *= 2
    return index


def by_tiles(rows, count):
    width = count * TILE_W
    whole = rows.astype(jnp.float32)
    lines = whole.shape[0] // width
    return [
        jnp.concatenate(
            [whole[r * width + w * TILE_W : r * width + (w + 1) * TILE_W] for r in range(lines)],
            axis=0,
        ).astype(rows.dtype)
        for w in range(count)
    ]


def by_rows(parts):
    parts = [part.astype(jnp.float32) for part in parts]
    lines = parts[0].shape[0] // TILE_W
    return jnp.concatenate(
        [part[r * TILE_W : (r + 1) * TILE_W] for r in range(lines) for part in parts], axis=0
    ).astype(jnp.bfloat16)


def fused_kernel(
    times, count, own_heads,
    q_hbm, k_hbm, v_hbm, win_hbm, out_ref,
    q_ref, k_ref, v_ref, win_ref, stage_kv, stage_q, kv, qs, outs, arrived, win,
    kv_send, kv_recv, q_send, q_recv, z_send, z_recv, o_send, o_recv, w_send, w_recv,
    in_sem, win_sem,
):
    t = lax.axis_index("temporal")
    me = lax.axis_index("spatial")
    part = q_ref.shape[0] // count
    peers = range(1, count)
    peer = [flipped(me, d) for d in range(count)]

    def rows_of(index):
        return pl.ds(pl.multiple_of(index * part, part), part)

    def columns_of(index, h):
        return pl.ds(pl.multiple_of((index * own_heads + h) * D_HEAD, D_HEAD), D_HEAD)

    def to(d):
        return {"spatial": peer[d]}

    def kv_copy(d, h, rows):
        return pltpu.make_async_remote_copy(
            src_ref=stage_kv.at[d - 1, h],
            dst_ref=kv.at[1, h, :, :, rows],
            send_sem=kv_send.at[d - 1, h],
            recv_sem=kv_recv.at[d - 1, h],
            device_id=to(d), device_id_type=MESH,
        )

    def q_copy(d, h, rows):
        return pltpu.make_async_remote_copy(
            src_ref=stage_q.at[d - 1, h],
            dst_ref=qs.at[h, :, rows],
            send_sem=q_send.at[d - 1, h],
            recv_sem=q_recv.at[d - 1, h],
            device_id=to(d), device_id_type=MESH,
        )

    def w_copy(d, slot):
        return pltpu.make_async_remote_copy(
            src_ref=win.at[slot],
            dst_ref=win.at[slot],
            send_sem=w_send.at[d - 1],
            recv_sem=w_recv.at[d - 1],
            device_id=to(d), device_id_type=MESH,
        )

    def z_copy(side, d, h):
        rows = rows_of(peer[d])
        return pltpu.make_async_remote_copy(
            src_ref=kv.at[1, h, :, :, rows],
            dst_ref=kv.at[2 * side, h, :, :, rows],
            send_sem=z_send.at[side, d, h],
            recv_sem=z_recv.at[side, d, h],
            device_id={"temporal": t + 1 - 2 * side}, device_id_type=MESH,
        )

    def o_copy(d, h, w):
        return pltpu.make_async_remote_copy(
            src_ref=outs.at[h, w, rows_of(peer[d])],
            dst_ref=arrived.at[d - 1, h, w],
            send_sem=o_send.at[d - 1, h, w],
            recv_sem=o_recv.at[d - 1, h, w],
            device_id=to(d), device_id_type=MESH,
        )

    def in_copy(i, d, h):
        here = columns_of(peer[d], h)
        return pltpu.make_async_copy(
            (k_hbm, v_hbm, q_hbm)[i].at[:, here],
            (k_ref, v_ref, q_ref)[i].at[:, here],
            in_sem.at[i, d, h],
        )

    for h in range(own_heads):
        for d in range(count):
            for i in range(2):
                in_copy(i, d, h).start()
    win_copy = pltpu.make_async_copy(win_hbm, win_ref, win_sem)
    win_copy.start()
    for h in range(own_heads):
        for d in range(count):
            in_copy(2, d, h).start()

    can_send = (t < times - 1, t > 0)
    can_take = (t > 0, t < times - 1)

    barrier = pltpu.get_barrier_semaphore()
    for d in peers:
        pl.semaphore_signal(barrier, inc=1, device_id=to(d), device_id_type=MESH)
    for side in range(2):
        @pl.when(can_send[side])
        def _(side=side):
            pl.semaphore_signal(
                barrier, inc=1, device_id={"temporal": t + 1 - 2 * side}, device_id_type=MESH
            )

    def lay_kv(d, h):
        for i, ref in enumerate((k_ref, v_ref)):
            in_copy(i, d, h).wait()
            for w, piece in enumerate(by_tiles(ref[:, columns_of(peer[d], h)], count)):
                if d:
                    stage_kv[d - 1, h, i, w] = piece
                else:
                    kv[1, h, i, w, rows_of(me)] = piece

    def lay_q(d, h):
        in_copy(2, d, h).wait()
        for w, piece in enumerate(by_tiles(q_ref[:, columns_of(peer[d], h)], count)):
            if d:
                stage_q[d - 1, h, w] = piece
            else:
                qs[h, w, rows_of(me)] = piece

    def forward(d, h):
        for side in range(2):
            @pl.when(can_send[side])
            def _(side=side):
                z_copy(side, d, h).start()

    lay_kv(0, 0)
    win_copy.wait()
    win[me] = jnp.zeros(win.shape[1:], win.dtype)
    win[me, 0:1, 0 : win_ref.shape[1]] = win_ref[...]
    for side in range(2):
        @pl.when(jnp.logical_not(can_take[side]))
        def _(side=side):
            kv[2 * side] = jnp.zeros(kv.shape[1:], kv.dtype)

    linked = can_send[0].astype(jnp.int32) + can_send[1].astype(jnp.int32)
    pl.semaphore_wait(barrier, count - 1 + linked)

    def early(d, h):
        return h == 0 or (h == 1 and d <= 1)

    forward(0, 0)
    for d in peers:
        lay_kv(d, 0)
        kv_copy(d, 0, rows_of(me)).start()
    for d in peers:
        w_copy(d, me).start()
    for h in range(1, own_heads):
        for d in range(count):
            lay_kv(d, h)
            if d == 0 and early(d, h):
                forward(d, h)
    for h in range(own_heads):
        for d in range(count):
            lay_q(d, h)

    for h in range(own_heads):
        for d in peers:
            kv_copy(d, h, rows_of(peer[d])).wait_recv()
            if early(d, h):
                forward(d, h)
            if h + 1 < own_heads:
                kv_copy(d, h + 1, rows_of(me)).start()
            else:
                q_copy(d, 0, rows_of(me)).start()
    for d in peers:
        w_copy(d, peer[d]).wait_recv()

    factor = math.log2(math.e) / math.sqrt(D_HEAD)
    for h in range(own_heads):
        for d in peers:
            q_copy(d, h, rows_of(peer[d])).wait_recv()
            if h + 1 < own_heads:
                q_copy(d, h + 1, rows_of(me)).start()
        for side in range(2):
            @pl.when(can_take[side])
            def _(side=side):
                for d in range(count):
                    z_copy(side, d, h).wait_recv()
        if h + 1 < own_heads:
            for d in range(count):
                if not early(d, h + 1):
                    forward(d, h + 1)
        for w in range(count):
            low, high = max(w - 1, 0), min(w + 2, count)
            query = qs[h, w]
            pattern = win[w, 0:1, :]
            wide = high - low
            keys = kv[:, h, 0, low:high].reshape(-1, D_HEAD)
            scores = lax.dot_general(
                query, keys, (((1,), (1,)), ((), ())), preferred_element_type=jnp.float32
            )
            blocks, limits, peak = [], [], None
            for i in range(3 * wide):
                p, c = i // wide, low + i % wide
                start = i * query.shape[0]
                halves = [
                    scores[:, j : j + LANES] for j in range(start, start + query.shape[0], LANES)
                ]
                entry = 9 * p + 3 + (c - w + 1)
                ok = pattern[:, entry : entry + 1] == 1
                if p != 1:
                    ok = jnp.logical_and(ok, can_take[p // 2])
                limit = jnp.where(ok, 0.0, jnp.inf).astype(jnp.float32)
                top = functools.reduce(jnp.maximum, halves) - limit
                peak = top if peak is None else jnp.maximum(peak, top)
                blocks.append(halves)
                limits.append(limit)
            peak = jnp.broadcast_to(jnp.max(peak, axis=1, keepdims=True), peak.shape)
            total, rounded = None, []
            for halves, limit in zip(blocks, limits):
                base = peak + limit
                for half in halves:
                    weights = jnp.exp2((half - base) * factor)
                    total = weights if total is None else total + weights
                    rounded.append(weights.astype(jnp.bfloat16))
            total = jnp.sum(total, axis=1, keepdims=True)
            mixed = jnp.dot(
                jnp.concatenate(rounded, axis=1),
                kv[:, h, 1, low:high].reshape(-1, D_HEAD),
                preferred_element_type=jnp.float32,
            )
            outs[h, w] = (mixed / total).astype(jnp.bfloat16)
            for d in peers:
                o_copy(d, h, w).start()

    for h in range(own_heads):
        out_ref[:, columns_of(me, h)] = by_rows([outs[h, w, rows_of(me)] for w in range(count)])
        for d in peers:
            for w in range(count):
                o_copy(d, h, w).wait_recv()
            out_ref[:, columns_of(peer[d], h)] = by_rows([arrived[d - 1, h, w] for w in range(count)])

    for h in range(own_heads):
        for d in peers:
            kv_copy(d, h, rows_of(me)).wait_send()
            q_copy(d, h, rows_of(me)).wait_send()
            for w in range(count):
                o_copy(d, h, w).wait_send()
        for side in range(2):
            @pl.when(can_send[side])
            def _(side=side):
                for d in range(count):
                    z_copy(side, d, h).wait_send()
    for d in peers:
        w_copy(d, me).wait_send()


def fused(queries, keys, values, window):
    count, times = lax.axis_size("spatial"), lax.axis_size("temporal")
    tokens, channels = queries.shape
    own = channels // (D_HEAD * count)
    part = tokens // count
    vmem = pl.BlockSpec(memory_space=pltpu.VMEM)
    dma = pltpu.SemaphoreType.DMA
    pairs = own * count * (3 * count - 2) * 3 * tokens * tokens * D_HEAD
    return pl.pallas_call(
        functools.partial(fused_kernel, times, count, own),
        out_shape=jax.ShapeDtypeStruct(queries.shape, queries.dtype),
        in_specs=[pl.BlockSpec(memory_space=pl.ANY)] * 4,
        out_specs=vmem,
        scratch_shapes=[
            pltpu.VMEM(queries.shape, jnp.bfloat16),
            pltpu.VMEM(queries.shape, jnp.bfloat16),
            pltpu.VMEM(queries.shape, jnp.bfloat16),
            pltpu.VMEM((1, window.size), jnp.int32),
            pltpu.VMEM((count - 1, own, 2, count, part, D_HEAD), jnp.bfloat16),
            pltpu.VMEM((count - 1, own, count, part, D_HEAD), jnp.bfloat16),
            pltpu.VMEM((3, own, 2, count, tokens, D_HEAD), jnp.bfloat16),
            pltpu.VMEM((own, count, tokens, D_HEAD), jnp.bfloat16),
            pltpu.VMEM((own, count, tokens, D_HEAD), jnp.bfloat16),
            pltpu.VMEM((count - 1, own, count, part, D_HEAD), jnp.bfloat16),
            pltpu.VMEM((count, 8, 128), jnp.int32),
            dma((count - 1, own)), dma((count - 1, own)),
            dma((count - 1, own)), dma((count - 1, own)),
            dma((2, count, own)), dma((2, count, own)),
            dma((count - 1, own, count)), dma((count - 1, own, count)),
            dma((count - 1,)), dma((count - 1,)),
            dma((3, count, own)), dma,
        ],
        compiler_params=pltpu.CompilerParams(
            collective_id=0, has_side_effects=True, vmem_limit_bytes=60 * 2**20
        ),
        cost_estimate=pl.CostEstimate(
            flops=4 * pairs, bytes_accessed=4 * tokens * channels * 2, transcendentals=pairs // D_HEAD
        ),
    )(queries, keys, values, window.reshape(1, -1))


def body(queries, keys, values, window):
    count = lax.axis_size("spatial")
    tokens, channels = queries.shape
    heads_here = channels // D_HEAD
    whole_tiles = window.shape[1] == 1 and window.shape[2] == 1 and tokens == TILE_T * TILE_H * TILE_W
    if whole_tiles and count & (count - 1) == 0 and heads_here % count == 0:
        return fused(queries, keys, values, window)
    return gathered(queries, keys, values, window)


def solution(mesh):
    return jax.shard_map(
        body,
        mesh=mesh,
        in_specs=(
            P(("temporal", "spatial"), "head"),
            P(("temporal", "spatial"), "head"),
            P(("temporal", "spatial"), "head"),
            P("temporal", None, "spatial", None),
        ),
        out_specs=P(("temporal", "spatial"), "head"),
        check_vma=False,
    )
```

```python
import functools
import math

import jax
import jax.numpy as jnp
from jax import lax
from jax.experimental import pallas as pl
from jax.experimental.pallas import tpu as pltpu
from jax.sharding import PartitionSpec as P

D_HEAD = 128
TILE_T = 4
TILE_H = 8
TILE_W = 8
LANES = 128
MESH = pl.DeviceIdType.MESH


def with_halo(array, sides, width):
    for axis, dim in sides:
        peers, length = (lax.axis_size(axis), array.shape[dim])
        up = [(i, (i + 1) % peers) for i in range(peers - 1)]
        down = [(j, i) for i, j in up]
        last = lax.slice_in_dim(array, length - width, length, axis=dim)
        initial = lax.slice_in_dim(array, 0, width, axis=dim)
        before = lax.ppermute(last, axis, up)
        after = lax.ppermute(initial, axis, down)
        array = jnp.concatenate([before, array, after], axis=dim)
    return array


def tile_mask(pattern, tile_row, first_row, window_rows, time_ok, width_ok):
    height_step = first_row - tile_row
    picked = [pattern[:, height_step + 1, :] == 1]
    chosen = jnp.stack(picked, axis=1)
    allowed = chosen & time_ok[:, None, None] & width_ok[None, None, :]
    return jnp.broadcast_to(
        allowed[:, None, :, None, :, None], (3, TILE_T, window_rows, TILE_H, 3, TILE_W)
    ).reshape(-1)


def attend(query_tile, key_window, value_window, key_ok):
    heads_here = query_tile.shape[1]
    group = min(2, heads_here)
    scale = 1.0 / math.sqrt(D_HEAD)
    pieces = []
    for head_start in range(0, heads_here, group):
        query_part = query_tile[:, head_start : head_start + group]
        key_part = key_window[:, head_start : head_start + group]
        value_part = value_window[:, head_start : head_start + group]
        scores = (
            jnp.einsum("qhd,khd->hqk", query_part, key_part, preferred_element_type=jnp.float32)
            * scale
        )
        scores = jnp.where(key_ok[None, None, :], scores, -jnp.inf)
        peak = jnp.max(scores, axis=-1, keepdims=True)
        weights = jnp.exp(scores - peak)
        total = jnp.sum(weights, axis=-1)
        attended_part = jnp.einsum(
            "hqk,khd->qhd",
            weights.astype(jnp.bfloat16),
            value_part,
            preferred_element_type=jnp.float32,
        )
        attended_part = attended_part / jnp.transpose(total)[:, :, None]
        pieces.append(attended_part.astype(jnp.bfloat16).reshape(attended_part.shape[0], -1))
    return jnp.concatenate(pieces, axis=1)


def gathered(queries, keys, values, window):
    space_count = lax.axis_size("spatial")
    time_count = lax.axis_size("temporal")
    tokens_dev, channels = queries.shape
    tile_rows = window.shape[1]
    height = tile_rows * TILE_H
    shard_rows = tokens_dev // (space_count * TILE_W)
    split = 1
    groups = space_count // split
    span = split * TILE_W
    part_channels = channels // split

    def to_blocks(tensor):
        shaped = tensor.reshape(shard_rows, groups, span, split, part_channels)
        return jnp.transpose(shaped, (3, 1, 0, 2, 4)).reshape(
            space_count, shard_rows, span, part_channels
        )

    def from_blocks(tensor):
        return tensor.reshape(TILE_T, height, span, part_channels)

    query_block, key_block, value_block = (
        lax.all_to_all(to_blocks(queries), "spatial", split_axis=0, concat_axis=0, tiled=True),
        lax.all_to_all(to_blocks(keys), "spatial", split_axis=0, concat_axis=0, tiled=True),
        lax.all_to_all(to_blocks(values), "spatial", split_axis=0, concat_axis=0, tiled=True),
    )
    add_key_block = from_blocks(key_block)
    add_value_block = from_blocks(value_block)
    paired = jnp.stack([add_key_block, add_value_block]).reshape(
        2, 1, TILE_T, height, split, TILE_W, part_channels
    )
    padded = with_halo(paired, (("temporal", 1), ("spatial", 4)), 1)
    query_block = from_blocks(query_block)
    column_base = lax.axis_index("spatial")
    offsets = jnp.arange(3, dtype=jnp.int32) - 1
    time_index = lax.axis_index("temporal") + offsets
    time_ok = (time_index >= 0) & (time_index < time_count)
    window_rows = min(3, tile_rows)
    heads_here = part_channels // D_HEAD
    width_index = column_base + 0 + offsets
    width_ok = (width_index >= 0) & (width_index < space_count)
    pattern_column = lax.dynamic_index_in_dim(window, 0, 2, keepdims=False)
    pattern_rows = pattern_column.reshape(tile_rows, 3, 3, 3)
    first_row = min(max(0 - 1, 0), tile_rows - window_rows)
    key_ok = tile_mask(pattern_rows[0], 0, first_row, window_rows, time_ok, width_ok)
    query_tile = query_block.reshape(-1, heads_here, D_HEAD)
    row_low = first_row * TILE_H
    row_high = row_low + window_rows * TILE_H
    key_window = padded[0, :, :, row_low:row_high, 0:3].reshape(-1, heads_here, D_HEAD)
    value_window = padded[1, :, :, row_low:row_high, 0:3].reshape(-1, heads_here, D_HEAD)
    attended_tile = attend(query_tile, key_window, value_window, key_ok)
    outputs = attended_tile.reshape(TILE_T, TILE_H, TILE_W, part_channels)
    result = outputs.reshape(space_count, shard_rows, span, part_channels)
    returned = lax.all_to_all(result, "spatial", split_axis=0, concat_axis=0, tiled=True)
    shaped = returned.reshape(split, groups, shard_rows, span, part_channels)
    return jnp.transpose(shaped, (2, 1, 3, 0, 4)).reshape(tokens_dev, channels)


def flipped(index, bits):
    bit = 1
    while bit <= bits:
        if bits & bit:
            index = index + bit - 2 * bit * ((index // bit) % 2)
        bit *= 2
    return index


def by_tiles(rows, count):
    width = count * TILE_W
    whole = rows.astype(jnp.float32)
    lines = whole.shape[0] // width
    return [
        jnp.concatenate(
            [whole[r * width + w * TILE_W : r * width + (w + 1) * TILE_W] for r in range(lines)],
            axis=0,
        ).astype(rows.dtype)
        for w in range(count)
    ]


def by_rows(parts):
    parts = [part.astype(jnp.float32) for part in parts]
    lines = parts[0].shape[0] // TILE_W
    return jnp.concatenate(
        [part[r * TILE_W : (r + 1) * TILE_W] for r in range(lines) for part in parts], axis=0
    ).astype(jnp.bfloat16)


def column_groups(count):
    first = min(2, count)
    return [(0, first)] + [(c, 1) for c in range(first, count)]


def fused_kernel(
    times, count, own_heads,
    q_hbm, k_hbm, v_hbm, win_hbm, out_ref,
    q_ref, k_ref, v_ref, win_ref, stage_kv, stage_q, kv, qs, outs, arrived, win,
    kv_send, kv_recv, q_send, q_recv, z_send, z_recv, o_send, o_recv, w_send, w_recv,
    in_sem, win_sem,
):
    t = lax.axis_index("temporal")
    me = lax.axis_index("spatial")
    part = q_ref.shape[0] // count
    peers = range(1, count)
    groups = column_groups(count)
    peer = [flipped(me, d) for d in range(count)]

    def rows_of(index):
        return pl.ds(pl.multiple_of(index * part, part), part)

    def columns_of(index, h):
        return pl.ds(pl.multiple_of((index * own_heads + h) * D_HEAD, D_HEAD), D_HEAD)

    def to(d):
        return {"spatial": peer[d]}

    def kv_copy(d, h, rows):
        return pltpu.make_async_remote_copy(
            src_ref=stage_kv.at[d - 1, h],
            dst_ref=kv.at[1, h, :, :, rows],
            send_sem=kv_send.at[d - 1, h],
            recv_sem=kv_recv.at[d - 1, h],
            device_id=to(d), device_id_type=MESH,
        )

    def q_copy(d, h, rows):
        return pltpu.make_async_remote_copy(
            src_ref=stage_q.at[d - 1, h],
            dst_ref=qs.at[h, :, rows],
            send_sem=q_send.at[d - 1, h],
            recv_sem=q_recv.at[d - 1, h],
            device_id=to(d), device_id_type=MESH,
        )

    def w_copy(d, slot):
        return pltpu.make_async_remote_copy(
            src_ref=win.at[slot],
            dst_ref=win.at[slot],
            send_sem=w_send.at[d - 1],
            recv_sem=w_recv.at[d - 1],
            device_id=to(d), device_id_type=MESH,
        )

    def z_copy(side, d, h, j):
        rows, tiles = rows_of(peer[d]), pl.ds(*groups[j])
        return pltpu.make_async_remote_copy(
            src_ref=kv.at[1, h, :, tiles, rows],
            dst_ref=kv.at[2 * side, h, :, tiles, rows],
            send_sem=z_send.at[side, d, h, j],
            recv_sem=z_recv.at[side, d, h, j],
            device_id={"temporal": t + 1 - 2 * side}, device_id_type=MESH,
        )

    def o_copy(d, h, w):
        return pltpu.make_async_remote_copy(
            src_ref=outs.at[h, w, rows_of(peer[d])],
            dst_ref=arrived.at[d - 1, h, w],
            send_sem=o_send.at[d - 1, h, w],
            recv_sem=o_recv.at[d - 1, h, w],
            device_id=to(d), device_id_type=MESH,
        )

    def in_copy(i, d, h):
        here = columns_of(peer[d], h)
        return pltpu.make_async_copy(
            (k_hbm, v_hbm, q_hbm)[i].at[:, here],
            (k_ref, v_ref, q_ref)[i].at[:, here],
            in_sem.at[i, d, h],
        )

    for h in range(own_heads):
        for d in range(count):
            for i in range(2):
                in_copy(i, d, h).start()
    win_copy = pltpu.make_async_copy(win_hbm, win_ref, win_sem)
    win_copy.start()
    for h in range(own_heads):
        for d in range(count):
            in_copy(2, d, h).start()

    can_send = (t < times - 1, t > 0)
    can_take = (t > 0, t < times - 1)

    barrier = pltpu.get_barrier_semaphore()
    for d in peers:
        pl.semaphore_signal(barrier, inc=1, device_id=to(d), device_id_type=MESH)
    for side in range(2):
        @pl.when(can_send[side])
        def _(side=side):
            pl.semaphore_signal(
                barrier, inc=1, device_id={"temporal": t + 1 - 2 * side}, device_id_type=MESH
            )

    def lay_kv(d, h):
        for i, ref in enumerate((k_ref, v_ref)):
            in_copy(i, d, h).wait()
            for w, piece in enumerate(by_tiles(ref[:, columns_of(peer[d], h)], count)):
                if d:
                    stage_kv[d - 1, h, i, w] = piece
                else:
                    kv[1, h, i, w, rows_of(me)] = piece

    def lay_q(d, h):
        in_copy(2, d, h).wait()
        for w, piece in enumerate(by_tiles(q_ref[:, columns_of(peer[d], h)], count)):
            if d:
                stage_q[d - 1, h, w] = piece
            else:
                qs[h, w, rows_of(me)] = piece

    def forward(d, h, these):
        for side in range(2):
            @pl.when(can_send[side])
            def _(side=side):
                for j in these:
                    z_copy(side, d, h, j).start()

    every = range(len(groups))

    lay_kv(0, 0)
    win_copy.wait()
    win[me] = jnp.zeros(win.shape[1:], win.dtype)
    win[me, 0:1, 0 : win_ref.shape[1]] = win_ref[...]
    for side in range(2):
        @pl.when(jnp.logical_not(can_take[side]))
        def _(side=side):
            kv[2 * side] = jnp.zeros(kv.shape[1:], kv.dtype)

    linked = can_send[0].astype(jnp.int32) + can_send[1].astype(jnp.int32)
    pl.semaphore_wait(barrier, count - 1 + linked)

    def early(d, h):
        return h == 0 or (h == 1 and d <= 1)

    forward(0, 0, every)
    for d in peers:
        lay_kv(d, 0)
        kv_copy(d, 0, rows_of(me)).start()
    for d in peers:
        w_copy(d, me).start()
    for h in range(1, own_heads):
        for d in range(count):
            lay_kv(d, h)
            if d == 0 and early(d, h):
                forward(d, h, every)
    for h in range(own_heads):
        for d in range(count):
            lay_q(d, h)

    for h in range(own_heads):
        for d in peers:
            kv_copy(d, h, rows_of(peer[d])).wait_recv()
            if early(d, h):
                forward(d, h, every)
            if h + 1 < own_heads:
                kv_copy(d, h + 1, rows_of(me)).start()
            else:
                q_copy(d, 0, rows_of(me)).start()
    for d in peers:
        w_copy(d, peer[d]).wait_recv()

    def bring_home(h):
        out_ref[:, columns_of(me, h)] = by_rows([outs[h, w, rows_of(me)] for w in range(count)])
        for d in peers:
            for w in range(count):
                o_copy(d, h, w).wait_recv()
            out_ref[:, columns_of(peer[d], h)] = by_rows([arrived[d - 1, h, w] for w in range(count)])

    factor = math.log2(math.e) / math.sqrt(D_HEAD)
    for h in range(own_heads):
        for d in peers:
            q_copy(d, h, rows_of(peer[d])).wait_recv()
            if h + 1 < own_heads:
                q_copy(d, h + 1, rows_of(me)).start()
        for w in range(count):
            if w < len(groups):
                for side in range(2):
                    @pl.when(can_take[side])
                    def _(side=side):
                        for d in range(count):
                            z_copy(side, d, h, w).wait_recv()
                if w == len(groups) - 1 and h + 1 < own_heads:
                    for d in range(count):
                        if not early(d, h + 1):
                            forward(d, h + 1, every[:2])
                if w == 0 and h:
                    for d in range(count):
                        if not early(d, h):
                            forward(d, h, every[2:])
                if w == len(groups) - 1 and h:
                    bring_home(h - 1)
            low, high = max(w - 1, 0), min(w + 2, count)
            query = qs[h, w]
            pattern = win[w, 0:1, :]
            wide = high - low
            keys = kv[:, h, 0, low:high].reshape(-1, D_HEAD)
            scores = lax.dot_general(
                query, keys, (((1,), (1,)), ((), ())), preferred_element_type=jnp.float32
            )
            blocks, limits, peak = [], [], None
            for i in range(3 * wide):
                p, c = i // wide, low + i % wide
                start = i * query.shape[0]
                halves = [
                    scores[:, j : j + LANES] for j in range(start, start + query.shape[0], LANES)
                ]
                entry = 9 * p + 3 + (c - w + 1)
                ok = pattern[:, entry : entry + 1] == 1
                if p != 1:
                    ok = jnp.logical_and(ok, can_take[p // 2])
                limit = jnp.where(ok, 0.0, jnp.inf).astype(jnp.float32)
                top = functools.reduce(jnp.maximum, halves) - limit
                peak = top if peak is None else jnp.maximum(peak, top)
                blocks.append(halves)
                limits.append(limit)
            peak = jnp.broadcast_to(jnp.max(peak, axis=1, keepdims=True), peak.shape)
            total, rounded = None, []
            for halves, limit in zip(blocks, limits):
                base = peak + limit
                for half in halves:
                    weights = jnp.exp2((half - base) * factor)
                    total = weights if total is None else total + weights
                    rounded.append(weights.astype(jnp.bfloat16))
            total = jnp.sum(total, axis=1, keepdims=True)
            mixed = jnp.dot(
                jnp.concatenate(rounded, axis=1),
                kv[:, h, 1, low:high].reshape(-1, D_HEAD),
                preferred_element_type=jnp.float32,
            )
            outs[h, w] = (mixed / total).astype(jnp.bfloat16)
            for d in peers:
                o_copy(d, h, w).start()

    bring_home(own_heads - 1)

    for h in range(own_heads):
        for d in peers:
            kv_copy(d, h, rows_of(me)).wait_send()
            q_copy(d, h, rows_of(me)).wait_send()
            for w in range(count):
                o_copy(d, h, w).wait_send()
        for side in range(2):
            @pl.when(can_send[side])
            def _(side=side):
                for d in range(count):
                    for j in every:
                        z_copy(side, d, h, j).wait_send()
    for d in peers:
        w_copy(d, me).wait_send()


def fused(queries, keys, values, window):
    count, times = lax.axis_size("spatial"), lax.axis_size("temporal")
    tokens, channels = queries.shape
    own = channels // (D_HEAD * count)
    part = tokens // count
    groups = len(column_groups(count))
    vmem = pl.BlockSpec(memory_space=pltpu.VMEM)
    dma = pltpu.SemaphoreType.DMA
    pairs = own * count * (3 * count - 2) * 3 * tokens * tokens * D_HEAD
    return pl.pallas_call(
        functools.partial(fused_kernel, times, count, own),
        out_shape=jax.ShapeDtypeStruct(queries.shape, queries.dtype),
        in_specs=[pl.BlockSpec(memory_space=pl.ANY)] * 4,
        out_specs=vmem,
        scratch_shapes=[
            pltpu.VMEM(queries.shape, jnp.bfloat16),
            pltpu.VMEM(queries.shape, jnp.bfloat16),
            pltpu.VMEM(queries.shape, jnp.bfloat16),
            pltpu.VMEM((1, window.size), jnp.int32),
            pltpu.VMEM((count - 1, own, 2, count, part, D_HEAD), jnp.bfloat16),
            pltpu.VMEM((count - 1, own, count, part, D_HEAD), jnp.bfloat16),
            pltpu.VMEM((3, own, 2, count, tokens, D_HEAD), jnp.bfloat16),
            pltpu.VMEM((own, count, tokens, D_HEAD), jnp.bfloat16),
            pltpu.VMEM((own, count, tokens, D_HEAD), jnp.bfloat16),
            pltpu.VMEM((count - 1, own, count, part, D_HEAD), jnp.bfloat16),
            pltpu.VMEM((count, 8, 128), jnp.int32),
            dma((count - 1, own)), dma((count - 1, own)),
            dma((count - 1, own)), dma((count - 1, own)),
            dma((2, count, own, groups)), dma((2, count, own, groups)),
            dma((count - 1, own, count)), dma((count - 1, own, count)),
            dma((count - 1,)), dma((count - 1,)),
            dma((3, count, own)), dma,
        ],
        compiler_params=pltpu.CompilerParams(
            collective_id=0, has_side_effects=True, vmem_limit_bytes=60 * 2**20
        ),
        cost_estimate=pl.CostEstimate(
            flops=4 * pairs, bytes_accessed=4 * tokens * channels * 2, transcendentals=pairs // D_HEAD
        ),
    )(queries, keys, values, window.reshape(1, -1))


def body(queries, keys, values, window):
    count = lax.axis_size("spatial")
    tokens, channels = queries.shape
    heads_here = channels // D_HEAD
    whole_tiles = window.shape[1] == 1 and window.shape[2] == 1 and tokens == TILE_T * TILE_H * TILE_W
    if whole_tiles and count & (count - 1) == 0 and heads_here % count == 0:
        return fused(queries, keys, values, window)
    return gathered(queries, keys, values, window)


def solution(mesh):
    return jax.shard_map(
        body,
        mesh=mesh,
        in_specs=(
            P(("temporal", "spatial"), "head"),
            P(("temporal", "spatial"), "head"),
            P(("temporal", "spatial"), "head"),
            P("temporal", None, "spatial", None),
        ),
        out_specs=P(("temporal", "spatial"), "head"),
        check_vma=False,
    )
```

```python
import functools
import math

import jax
import jax.numpy as jnp
from jax import lax
from jax.experimental import pallas as pl
from jax.experimental.pallas import tpu as pltpu
from jax.sharding import PartitionSpec as P

D_HEAD = 128
TILE_T = 4
TILE_H = 8
TILE_W = 8
LANES = 128
MESH = pl.DeviceIdType.MESH


def with_halo(array, sides, width):
    for axis, dim in sides:
        peers, length = (lax.axis_size(axis), array.shape[dim])
        up = [(i, (i + 1) % peers) for i in range(peers - 1)]
        down = [(j, i) for i, j in up]
        last = lax.slice_in_dim(array, length - width, length, axis=dim)
        initial = lax.slice_in_dim(array, 0, width, axis=dim)
        before = lax.ppermute(last, axis, up)
        after = lax.ppermute(initial, axis, down)
        array = jnp.concatenate([before, array, after], axis=dim)
    return array


def tile_mask(pattern, tile_row, first_row, window_rows, time_ok, width_ok):
    height_step = first_row - tile_row
    picked = [pattern[:, height_step + 1, :] == 1]
    chosen = jnp.stack(picked, axis=1)
    allowed = chosen & time_ok[:, None, None] & width_ok[None, None, :]
    return jnp.broadcast_to(
        allowed[:, None, :, None, :, None], (3, TILE_T, window_rows, TILE_H, 3, TILE_W)
    ).reshape(-1)


def attend(query_tile, key_window, value_window, key_ok):
    heads_here = query_tile.shape[1]
    group = min(2, heads_here)
    scale = 1.0 / math.sqrt(D_HEAD)
    pieces = []
    for head_start in range(0, heads_here, group):
        query_part = query_tile[:, head_start : head_start + group]
        key_part = key_window[:, head_start : head_start + group]
        value_part = value_window[:, head_start : head_start + group]
        scores = (
            jnp.einsum("qhd,khd->hqk", query_part, key_part, preferred_element_type=jnp.float32)
            * scale
        )
        scores = jnp.where(key_ok[None, None, :], scores, -jnp.inf)
        peak = jnp.max(scores, axis=-1, keepdims=True)
        weights = jnp.exp(scores - peak)
        total = jnp.sum(weights, axis=-1)
        attended_part = jnp.einsum(
            "hqk,khd->qhd",
            weights.astype(jnp.bfloat16),
            value_part,
            preferred_element_type=jnp.float32,
        )
        attended_part = attended_part / jnp.transpose(total)[:, :, None]
        pieces.append(attended_part.astype(jnp.bfloat16).reshape(attended_part.shape[0], -1))
    return jnp.concatenate(pieces, axis=1)


def gathered(queries, keys, values, window):
    space_count = lax.axis_size("spatial")
    time_count = lax.axis_size("temporal")
    tokens_dev, channels = queries.shape
    tile_rows = window.shape[1]
    height = tile_rows * TILE_H
    shard_rows = tokens_dev // (space_count * TILE_W)
    split = 1
    groups = space_count // split
    span = split * TILE_W
    part_channels = channels // split

    def to_blocks(tensor):
        shaped = tensor.reshape(shard_rows, groups, span, split, part_channels)
        return jnp.transpose(shaped, (3, 1, 0, 2, 4)).reshape(
            space_count, shard_rows, span, part_channels
        )

    def from_blocks(tensor):
        return tensor.reshape(TILE_T, height, span, part_channels)

    query_block, key_block, value_block = (
        lax.all_to_all(to_blocks(queries), "spatial", split_axis=0, concat_axis=0, tiled=True),
        lax.all_to_all(to_blocks(keys), "spatial", split_axis=0, concat_axis=0, tiled=True),
        lax.all_to_all(to_blocks(values), "spatial", split_axis=0, concat_axis=0, tiled=True),
    )
    add_key_block = from_blocks(key_block)
    add_value_block = from_blocks(value_block)
    paired = jnp.stack([add_key_block, add_value_block]).reshape(
        2, 1, TILE_T, height, split, TILE_W, part_channels
    )
    padded = with_halo(paired, (("temporal", 1), ("spatial", 4)), 1)
    query_block = from_blocks(query_block)
    column_base = lax.axis_index("spatial")
    offsets = jnp.arange(3, dtype=jnp.int32) - 1
    time_index = lax.axis_index("temporal") + offsets
    time_ok = (time_index >= 0) & (time_index < time_count)
    window_rows = min(3, tile_rows)
    heads_here = part_channels // D_HEAD
    width_index = column_base + 0 + offsets
    width_ok = (width_index >= 0) & (width_index < space_count)
    pattern_column = lax.dynamic_index_in_dim(window, 0, 2, keepdims=False)
    pattern_rows = pattern_column.reshape(tile_rows, 3, 3, 3)
    first_row = min(max(0 - 1, 0), tile_rows - window_rows)
    key_ok = tile_mask(pattern_rows[0], 0, first_row, window_rows, time_ok, width_ok)
    query_tile = query_block.reshape(-1, heads_here, D_HEAD)
    row_low = first_row * TILE_H
    row_high = row_low + window_rows * TILE_H
    key_window = padded[0, :, :, row_low:row_high, 0:3].reshape(-1, heads_here, D_HEAD)
    value_window = padded[1, :, :, row_low:row_high, 0:3].reshape(-1, heads_here, D_HEAD)
    attended_tile = attend(query_tile, key_window, value_window, key_ok)
    outputs = attended_tile.reshape(TILE_T, TILE_H, TILE_W, part_channels)
    result = outputs.reshape(space_count, shard_rows, span, part_channels)
    returned = lax.all_to_all(result, "spatial", split_axis=0, concat_axis=0, tiled=True)
    shaped = returned.reshape(split, groups, shard_rows, span, part_channels)
    return jnp.transpose(shaped, (2, 1, 3, 0, 4)).reshape(tokens_dev, channels)


def flipped(index, bits):
    bit = 1
    while bit <= bits:
        if bits & bit:
            index = index + bit - 2 * bit * ((index // bit) % 2)
        bit *= 2
    return index


def by_tiles(rows, count):
    width = count * TILE_W
    whole = rows.astype(jnp.float32)
    lines = whole.shape[0] // width
    return [
        jnp.concatenate(
            [whole[r * width + w * TILE_W : r * width + (w + 1) * TILE_W] for r in range(lines)],
            axis=0,
        ).astype(rows.dtype)
        for w in range(count)
    ]


def by_rows(parts):
    parts = [part.astype(jnp.float32) for part in parts]
    lines = parts[0].shape[0] // TILE_W
    return jnp.concatenate(
        [part[r * TILE_W : (r + 1) * TILE_W] for r in range(lines) for part in parts], axis=0
    ).astype(jnp.bfloat16)


def fused_kernel(
    times, count, own_heads,
    q_hbm, k_hbm, v_hbm, win_hbm, out_ref,
    q_ref, k_ref, v_ref, win_ref, stage_kv, stage_q, kv, qs, outs, arrived, win,
    kv_send, kv_recv, q_send, q_recv, z_send, z_recv, o_send, o_recv, w_send, w_recv,
    in_sem, win_sem,
):
    t = lax.axis_index("temporal")
    me = lax.axis_index("spatial")
    part = q_ref.shape[0] // count
    peers = range(1, count)
    peer = [flipped(me, d) for d in range(count)]

    def rows_of(index):
        return pl.ds(pl.multiple_of(index * part, part), part)

    def columns_of(index, h):
        return pl.ds(pl.multiple_of((index * own_heads + h) * D_HEAD, D_HEAD), D_HEAD)

    def to(d):
        return {"spatial": peer[d]}

    def kv_copy(d, h, rows):
        return pltpu.make_async_remote_copy(
            src_ref=stage_kv.at[d - 1, h],
            dst_ref=kv.at[1, h, :, :, rows],
            send_sem=kv_send.at[d - 1, h],
            recv_sem=kv_recv.at[d - 1, h],
            device_id=to(d), device_id_type=MESH,
        )

    def q_copy(d, h, rows):
        return pltpu.make_async_remote_copy(
            src_ref=stage_q.at[d - 1, h],
            dst_ref=qs.at[h, :, rows],
            send_sem=q_send.at[d - 1, h],
            recv_sem=q_recv.at[d - 1, h],
            device_id=to(d), device_id_type=MESH,
        )

    def w_copy(d, slot):
        return pltpu.make_async_remote_copy(
            src_ref=win.at[slot],
            dst_ref=win.at[slot],
            send_sem=w_send.at[d - 1],
            recv_sem=w_recv.at[d - 1],
            device_id=to(d), device_id_type=MESH,
        )

    def z_copy(side, d, h):
        rows = rows_of(peer[d])
        return pltpu.make_async_remote_copy(
            src_ref=kv.at[1, h, :, :, rows],
            dst_ref=kv.at[2 * side, h, :, :, rows],
            send_sem=z_send.at[side, d, h],
            recv_sem=z_recv.at[side, d, h],
            device_id={"temporal": t + 1 - 2 * side}, device_id_type=MESH,
        )

    def o_copy(d, h, w):
        return pltpu.make_async_remote_copy(
            src_ref=outs.at[h, w, rows_of(peer[d])],
            dst_ref=arrived.at[d - 1, h, w],
            send_sem=o_send.at[d - 1, h, w],
            recv_sem=o_recv.at[d - 1, h, w],
            device_id=to(d), device_id_type=MESH,
        )

    def in_copy(i, d, h):
        here = columns_of(peer[d], h)
        return pltpu.make_async_copy(
            (k_hbm, v_hbm, q_hbm)[i].at[:, here],
            (k_ref, v_ref, q_ref)[i].at[:, here],
            in_sem.at[i, d, h],
        )

    for h in range(own_heads):
        for d in range(count):
            for i in range(2):
                in_copy(i, d, h).start()
    win_copy = pltpu.make_async_copy(win_hbm, win_ref, win_sem)
    win_copy.start()
    for h in range(own_heads):
        for d in range(count):
            in_copy(2, d, h).start()

    can_send = (t < times - 1, t > 0)
    can_take = (t > 0, t < times - 1)

    barrier = pltpu.get_barrier_semaphore()
    for d in peers:
        pl.semaphore_signal(barrier, inc=1, device_id=to(d), device_id_type=MESH)
    for side in range(2):
        @pl.when(can_send[side])
        def _(side=side):
            pl.semaphore_signal(
                barrier, inc=1, device_id={"temporal": t + 1 - 2 * side}, device_id_type=MESH
            )

    def lay_kv(d, h):
        for i, ref in enumerate((k_ref, v_ref)):
            in_copy(i, d, h).wait()
            for w, piece in enumerate(by_tiles(ref[:, columns_of(peer[d], h)], count)):
                if d:
                    stage_kv[d - 1, h, i, w] = piece
                else:
                    kv[1, h, i, w, rows_of(me)] = piece

    def lay_q(d, h):
        in_copy(2, d, h).wait()
        for w, piece in enumerate(by_tiles(q_ref[:, columns_of(peer[d], h)], count)):
            if d:
                stage_q[d - 1, h, w] = piece
            else:
                qs[h, w, rows_of(me)] = piece

    def forward(d, h):
        for side in range(2):
            @pl.when(can_send[side])
            def _(side=side):
                z_copy(side, d, h).start()

    lay_kv(0, 0)
    win_copy.wait()
    win[me] = jnp.zeros(win.shape[1:], win.dtype)
    win[me, 0:1, 0 : win_ref.shape[1]] = win_ref[...]
    for side in range(2):
        @pl.when(jnp.logical_not(can_take[side]))
        def _(side=side):
            kv[2 * side] = jnp.zeros(kv.shape[1:], kv.dtype)

    linked = can_send[0].astype(jnp.int32) + can_send[1].astype(jnp.int32)
    pl.semaphore_wait(barrier, count - 1 + linked)

    def early(d, h):
        return h == 0 or (h == 1 and d <= 1)

    forward(0, 0)
    for d in peers:
        lay_kv(d, 0)
        kv_copy(d, 0, rows_of(me)).start()
    for d in peers:
        w_copy(d, me).start()
    for h in range(1, own_heads):
        for d in range(count):
            lay_kv(d, h)
            if d == 0 and early(d, h):
                forward(d, h)
    for h in range(own_heads):
        for d in range(count):
            lay_q(d, h)

    for h in range(own_heads):
        for d in peers:
            kv_copy(d, h, rows_of(peer[d])).wait_recv()
            if early(d, h):
                forward(d, h)
            if h + 1 < own_heads:
                kv_copy(d, h + 1, rows_of(me)).start()
            else:
                q_copy(d, 0, rows_of(me)).start()
    for d in peers:
        w_copy(d, peer[d]).wait_recv()

    def bring_home(h):
        out_ref[:, columns_of(me, h)] = by_rows([outs[h, w, rows_of(me)] for w in range(count)])
        for d in peers:
            for w in range(count):
                o_copy(d, h, w).wait_recv()
            out_ref[:, columns_of(peer[d], h)] = by_rows([arrived[d - 1, h, w] for w in range(count)])

    def limit_of(w, p, c):
        entry = 9 * p + 3 + (c - w + 1)
        ok = win[w, 0:1, entry : entry + 1] == 1
        if p != 1:
            ok = jnp.logical_and(ok, can_take[p // 2])
        return jnp.where(ok, 0.0, jnp.inf).astype(jnp.float32)

    def score(h, w, p, c):
        return lax.dot_general(
            qs[h, w], kv[p, h, 0, c], (((1,), (1,)), ((), ())), preferred_element_type=jnp.float32
        )

    def halves_of(block):
        return [block[:, j : j + LANES] for j in range(0, block.shape[1], LANES)]

    factor = math.log2(math.e) / math.sqrt(D_HEAD)
    near = [range(max(w - 1, 0), min(w + 2, count)) for w in range(count)]
    for h in range(own_heads):
        for d in peers:
            q_copy(d, h, rows_of(peer[d])).wait_recv()
            if h + 1 < own_heads:
                q_copy(d, h + 1, rows_of(me)).start()
        scores = [{(1, c): score(h, w, 1, c) for c in near[w]} for w in range(count)]
        if h:
            bring_home(h - 1)
        for side in range(2):
            @pl.when(can_take[side])
            def _(side=side):
                for d in range(count):
                    z_copy(side, d, h).wait_recv()
        if h + 1 < own_heads:
            for d in range(count):
                if not early(d, h + 1):
                    forward(d, h + 1)

        later = [[(p, c) for p in (0, 2) for c in near[w]] for w in range(count)]
        for spot in later[0]:
            scores[0][spot] = score(h, 0, *spot)
        for w in range(count):
            spots = [(p, c) for p in range(3) for c in near[w]]
            limits = {spot: limit_of(w, *spot) for spot in spots}
            tops = [
                functools.reduce(jnp.maximum, halves_of(scores[w][spot])) - limits[spot]
                for spot in spots
            ]
            peak = functools.reduce(jnp.maximum, tops)
            peak = jnp.broadcast_to(jnp.max(peak, axis=1, keepdims=True), peak.shape)
            pending = list(later[w + 1]) if w + 1 < count else []
            total, mixed = None, None
            for spot in spots:
                base = peak + limits[spot]
                rounded = []
                for half in halves_of(scores[w].pop(spot)):
                    weights = jnp.exp2((half - base) * factor)
                    total = weights if total is None else total + weights
                    rounded.append(weights.astype(jnp.bfloat16))
                if pending:
                    ahead = pending.pop(0)
                    scores[w + 1][ahead] = score(h, w + 1, *ahead)
                product = jnp.dot(
                    jnp.concatenate(rounded, axis=1), kv[spot[0], h, 1, spot[1]],
                    preferred_element_type=jnp.float32,
                )
                mixed = product if mixed is None else mixed + product
            for ahead in pending:
                scores[w + 1][ahead] = score(h, w + 1, *ahead)
            total = jnp.sum(total, axis=1, keepdims=True)
            outs[h, w] = (mixed / total).astype(jnp.bfloat16)
            for d in peers:
                o_copy(d, h, w).start()
    bring_home(own_heads - 1)

    for h in range(own_heads):
        for d in peers:
            kv_copy(d, h, rows_of(me)).wait_send()
            q_copy(d, h, rows_of(me)).wait_send()
            for w in range(count):
                o_copy(d, h, w).wait_send()
        for side in range(2):
            @pl.when(can_send[side])
            def _(side=side):
                for d in range(count):
                    z_copy(side, d, h).wait_send()
    for d in peers:
        w_copy(d, me).wait_send()


def fused(queries, keys, values, window):
    count, times = lax.axis_size("spatial"), lax.axis_size("temporal")
    tokens, channels = queries.shape
    own = channels // (D_HEAD * count)
    part = tokens // count
    vmem = pl.BlockSpec(memory_space=pltpu.VMEM)
    dma = pltpu.SemaphoreType.DMA
    pairs = own * count * (3 * count - 2) * 3 * tokens * tokens * D_HEAD
    return pl.pallas_call(
        functools.partial(fused_kernel, times, count, own),
        out_shape=jax.ShapeDtypeStruct(queries.shape, queries.dtype),
        in_specs=[pl.BlockSpec(memory_space=pl.ANY)] * 4,
        out_specs=vmem,
        scratch_shapes=[
            pltpu.VMEM(queries.shape, jnp.bfloat16),
            pltpu.VMEM(queries.shape, jnp.bfloat16),
            pltpu.VMEM(queries.shape, jnp.bfloat16),
            pltpu.VMEM((1, window.size), jnp.int32),
            pltpu.VMEM((count - 1, own, 2, count, part, D_HEAD), jnp.bfloat16),
            pltpu.VMEM((count - 1, own, count, part, D_HEAD), jnp.bfloat16),
            pltpu.VMEM((3, own, 2, count, tokens, D_HEAD), jnp.bfloat16),
            pltpu.VMEM((own, count, tokens, D_HEAD), jnp.bfloat16),
            pltpu.VMEM((own, count, tokens, D_HEAD), jnp.bfloat16),
            pltpu.VMEM((count - 1, own, count, part, D_HEAD), jnp.bfloat16),
            pltpu.VMEM((count, 8, 128), jnp.int32),
            dma((count - 1, own)), dma((count - 1, own)),
            dma((count - 1, own)), dma((count - 1, own)),
            dma((2, count, own)), dma((2, count, own)),
            dma((count - 1, own, count)), dma((count - 1, own, count)),
            dma((count - 1,)), dma((count - 1,)),
            dma((3, count, own)), dma,
        ],
        compiler_params=pltpu.CompilerParams(
            collective_id=0, has_side_effects=True, vmem_limit_bytes=60 * 2**20
        ),
        cost_estimate=pl.CostEstimate(
            flops=4 * pairs, bytes_accessed=4 * tokens * channels * 2, transcendentals=pairs // D_HEAD
        ),
    )(queries, keys, values, window.reshape(1, -1))


def body(queries, keys, values, window):
    count = lax.axis_size("spatial")
    tokens, channels = queries.shape
    heads_here = channels // D_HEAD
    whole_tiles = window.shape[1] == 1 and window.shape[2] == 1 and tokens == TILE_T * TILE_H * TILE_W
    if whole_tiles and count & (count - 1) == 0 and heads_here % count == 0:
        return fused(queries, keys, values, window)
    return gathered(queries, keys, values, window)


def solution(mesh):
    return jax.shard_map(
        body,
        mesh=mesh,
        in_specs=(
            P(("temporal", "spatial"), "head"),
            P(("temporal", "spatial"), "head"),
            P(("temporal", "spatial"), "head"),
            P("temporal", None, "spatial", None),
        ),
        out_specs=P(("temporal", "spatial"), "head"),
        check_vma=False,
    )
```

```python
import functools
import math

import jax
import jax.numpy as jnp
from jax import lax
from jax.experimental import pallas as pl
from jax.experimental.pallas import tpu as pltpu
from jax.sharding import PartitionSpec as P

D_HEAD = 128
TILE_T = 4
TILE_H = 8
TILE_W = 8
LANES = 128
MESH = pl.DeviceIdType.MESH


def with_halo(array, sides, width):
    for axis, dim in sides:
        peers, length = (lax.axis_size(axis), array.shape[dim])
        up = [(i, (i + 1) % peers) for i in range(peers - 1)]
        down = [(j, i) for i, j in up]
        last = lax.slice_in_dim(array, length - width, length, axis=dim)
        initial = lax.slice_in_dim(array, 0, width, axis=dim)
        before = lax.ppermute(last, axis, up)
        after = lax.ppermute(initial, axis, down)
        array = jnp.concatenate([before, array, after], axis=dim)
    return array


def tile_mask(pattern, tile_row, first_row, window_rows, time_ok, width_ok):
    height_step = first_row - tile_row
    picked = [pattern[:, height_step + 1, :] == 1]
    chosen = jnp.stack(picked, axis=1)
    allowed = chosen & time_ok[:, None, None] & width_ok[None, None, :]
    return jnp.broadcast_to(
        allowed[:, None, :, None, :, None], (3, TILE_T, window_rows, TILE_H, 3, TILE_W)
    ).reshape(-1)


def attend(query_tile, key_window, value_window, key_ok):
    heads_here = query_tile.shape[1]
    group = min(2, heads_here)
    scale = 1.0 / math.sqrt(D_HEAD)
    pieces = []
    for head_start in range(0, heads_here, group):
        query_part = query_tile[:, head_start : head_start + group]
        key_part = key_window[:, head_start : head_start + group]
        value_part = value_window[:, head_start : head_start + group]
        scores = (
            jnp.einsum("qhd,khd->hqk", query_part, key_part, preferred_element_type=jnp.float32)
            * scale
        )
        scores = jnp.where(key_ok[None, None, :], scores, -jnp.inf)
        peak = jnp.max(scores, axis=-1, keepdims=True)
        weights = jnp.exp(scores - peak)
        total = jnp.sum(weights, axis=-1)
        attended_part = jnp.einsum(
            "hqk,khd->qhd",
            weights.astype(jnp.bfloat16),
            value_part,
            preferred_element_type=jnp.float32,
        )
        attended_part = attended_part / jnp.transpose(total)[:, :, None]
        pieces.append(attended_part.astype(jnp.bfloat16).reshape(attended_part.shape[0], -1))
    return jnp.concatenate(pieces, axis=1)


def gathered(queries, keys, values, window):
    space_count = lax.axis_size("spatial")
    time_count = lax.axis_size("temporal")
    tokens_dev, channels = queries.shape
    tile_rows = window.shape[1]
    height = tile_rows * TILE_H
    shard_rows = tokens_dev // (space_count * TILE_W)
    split = 1
    groups = space_count // split
    span = split * TILE_W
    part_channels = channels // split

    def to_blocks(tensor):
        shaped = tensor.reshape(shard_rows, groups, span, split, part_channels)
        return jnp.transpose(shaped, (3, 1, 0, 2, 4)).reshape(
            space_count, shard_rows, span, part_channels
        )

    def from_blocks(tensor):
        return tensor.reshape(TILE_T, height, span, part_channels)

    query_block, key_block, value_block = (
        lax.all_to_all(to_blocks(queries), "spatial", split_axis=0, concat_axis=0, tiled=True),
        lax.all_to_all(to_blocks(keys), "spatial", split_axis=0, concat_axis=0, tiled=True),
        lax.all_to_all(to_blocks(values), "spatial", split_axis=0, concat_axis=0, tiled=True),
    )
    add_key_block = from_blocks(key_block)
    add_value_block = from_blocks(value_block)
    paired = jnp.stack([add_key_block, add_value_block]).reshape(
        2, 1, TILE_T, height, split, TILE_W, part_channels
    )
    padded = with_halo(paired, (("temporal", 1), ("spatial", 4)), 1)
    query_block = from_blocks(query_block)
    column_base = lax.axis_index("spatial")
    offsets = jnp.arange(3, dtype=jnp.int32) - 1
    time_index = lax.axis_index("temporal") + offsets
    time_ok = (time_index >= 0) & (time_index < time_count)
    window_rows = min(3, tile_rows)
    heads_here = part_channels // D_HEAD
    width_index = column_base + 0 + offsets
    width_ok = (width_index >= 0) & (width_index < space_count)
    pattern_column = lax.dynamic_index_in_dim(window, 0, 2, keepdims=False)
    pattern_rows = pattern_column.reshape(tile_rows, 3, 3, 3)
    first_row = min(max(0 - 1, 0), tile_rows - window_rows)
    key_ok = tile_mask(pattern_rows[0], 0, first_row, window_rows, time_ok, width_ok)
    query_tile = query_block.reshape(-1, heads_here, D_HEAD)
    row_low = first_row * TILE_H
    row_high = row_low + window_rows * TILE_H
    key_window = padded[0, :, :, row_low:row_high, 0:3].reshape(-1, heads_here, D_HEAD)
    value_window = padded[1, :, :, row_low:row_high, 0:3].reshape(-1, heads_here, D_HEAD)
    attended_tile = attend(query_tile, key_window, value_window, key_ok)
    outputs = attended_tile.reshape(TILE_T, TILE_H, TILE_W, part_channels)
    result = outputs.reshape(space_count, shard_rows, span, part_channels)
    returned = lax.all_to_all(result, "spatial", split_axis=0, concat_axis=0, tiled=True)
    shaped = returned.reshape(split, groups, shard_rows, span, part_channels)
    return jnp.transpose(shaped, (2, 1, 3, 0, 4)).reshape(tokens_dev, channels)


def flipped(index, bits):
    bit = 1
    while bit <= bits:
        if bits & bit:
            index = index + bit - 2 * bit * ((index // bit) % 2)
        bit *= 2
    return index


def by_tiles(rows, count):
    width = count * TILE_W
    whole = rows.astype(jnp.float32)
    lines = whole.shape[0] // width
    return [
        jnp.concatenate(
            [whole[r * width + w * TILE_W : r * width + (w + 1) * TILE_W] for r in range(lines)],
            axis=0,
        ).astype(rows.dtype)
        for w in range(count)
    ]


def by_rows(parts):
    parts = [part.astype(jnp.float32) for part in parts]
    lines = parts[0].shape[0] // TILE_W
    return jnp.concatenate(
        [part[r * TILE_W : (r + 1) * TILE_W] for r in range(lines) for part in parts], axis=0
    ).astype(jnp.bfloat16)


def fused_kernel(
    times, count, own_heads,
    q_hbm, k_hbm, v_hbm, win_hbm, out_ref,
    q_ref, k_ref, v_ref, win_ref, stage_kv, stage_q, kv, qs, outs, arrived, win,
    kv_send, kv_recv, q_send, q_recv, z_send, z_recv, o_send, o_recv, w_send, w_recv,
    in_sem, win_sem,
):
    t = lax.axis_index("temporal")
    me = lax.axis_index("spatial")
    part = q_ref.shape[0] // count
    peers = range(1, count)
    peer = [flipped(me, d) for d in range(count)]

    def rows_of(index):
        return pl.ds(pl.multiple_of(index * part, part), part)

    def columns_of(index, h):
        return pl.ds(pl.multiple_of((index * own_heads + h) * D_HEAD, D_HEAD), D_HEAD)

    def to(d):
        return {"spatial": peer[d]}

    def kv_copy(d, h, shard):
        return pltpu.make_async_remote_copy(
            src_ref=stage_kv.at[d - 1, h],
            dst_ref=kv.at[1, h, shard],
            send_sem=kv_send.at[d - 1, h],
            recv_sem=kv_recv.at[d - 1, h],
            device_id=to(d), device_id_type=MESH,
        )

    def q_copy(d, h, shard):
        return pltpu.make_async_remote_copy(
            src_ref=stage_q.at[d - 1, h],
            dst_ref=qs.at[h, shard],
            send_sem=q_send.at[d - 1, h],
            recv_sem=q_recv.at[d - 1, h],
            device_id=to(d), device_id_type=MESH,
        )

    def w_copy(d, slot):
        return pltpu.make_async_remote_copy(
            src_ref=win.at[slot],
            dst_ref=win.at[slot],
            send_sem=w_send.at[d - 1],
            recv_sem=w_recv.at[d - 1],
            device_id=to(d), device_id_type=MESH,
        )

    def z_copy(side, d, h):
        return pltpu.make_async_remote_copy(
            src_ref=kv.at[1, h, peer[d]],
            dst_ref=kv.at[2 * side, h, peer[d]],
            send_sem=z_send.at[side, d, h],
            recv_sem=z_recv.at[side, d, h],
            device_id={"temporal": t + 1 - 2 * side}, device_id_type=MESH,
        )

    def o_copy(d, h, w):
        return pltpu.make_async_remote_copy(
            src_ref=outs.at[h, w, rows_of(peer[d])],
            dst_ref=arrived.at[d - 1, h, w],
            send_sem=o_send.at[d - 1, h, w],
            recv_sem=o_recv.at[d - 1, h, w],
            device_id=to(d), device_id_type=MESH,
        )

    def in_copy(i, d, h):
        here = columns_of(peer[d], h)
        return pltpu.make_async_copy(
            (k_hbm, v_hbm, q_hbm)[i].at[:, here],
            (k_ref, v_ref, q_ref)[i].at[:, here],
            in_sem.at[i, d, h],
        )

    for h in range(own_heads):
        for d in range(count):
            for i in range(2):
                in_copy(i, d, h).start()
    win_copy = pltpu.make_async_copy(win_hbm, win_ref, win_sem)
    win_copy.start()
    for h in range(own_heads):
        for d in range(count):
            in_copy(2, d, h).start()

    can_send = (t < times - 1, t > 0)
    can_take = (t > 0, t < times - 1)

    barrier = pltpu.get_barrier_semaphore()
    for d in peers:
        pl.semaphore_signal(barrier, inc=1, device_id=to(d), device_id_type=MESH)
    for side in range(2):
        @pl.when(can_send[side])
        def _(side=side):
            pl.semaphore_signal(
                barrier, inc=1, device_id={"temporal": t + 1 - 2 * side}, device_id_type=MESH
            )

    def lay_kv(d, h):
        for i, ref in enumerate((k_ref, v_ref)):
            in_copy(i, d, h).wait()
            for w, piece in enumerate(by_tiles(ref[:, columns_of(peer[d], h)], count)):
                if d:
                    stage_kv[d - 1, h, i, w] = piece
                else:
                    kv[1, h, me, i, w] = piece

    def lay_q(d, h):
        in_copy(2, d, h).wait()
        for w, piece in enumerate(by_tiles(q_ref[:, columns_of(peer[d], h)], count)):
            if d:
                stage_q[d - 1, h, w] = piece
            else:
                qs[h, me, w] = piece

    def forward(d, h):
        for side in range(2):
            @pl.when(can_send[side])
            def _(side=side):
                z_copy(side, d, h).start()

    lay_kv(0, 0)
    win_copy.wait()
    win[me] = jnp.zeros(win.shape[1:], win.dtype)
    win[me, 0:1, 0 : win_ref.shape[1]] = win_ref[...]
    for side in range(2):
        @pl.when(jnp.logical_not(can_take[side]))
        def _(side=side):
            kv[2 * side] = jnp.zeros(kv.shape[1:], kv.dtype)

    linked = can_send[0].astype(jnp.int32) + can_send[1].astype(jnp.int32)
    pl.semaphore_wait(barrier, count - 1 + linked)

    def early(d, h):
        return h == 0 or (h == 1 and d <= 1)

    forward(0, 0)
    for d in peers:
        lay_kv(d, 0)
        kv_copy(d, 0, me).start()
    for d in peers:
        w_copy(d, me).start()
    for h in range(1, own_heads):
        for d in range(count):
            lay_kv(d, h)
            if d == 0 and early(d, h):
                forward(d, h)
    for h in range(own_heads):
        for d in range(count):
            lay_q(d, h)

    for h in range(own_heads):
        for d in peers:
            kv_copy(d, h, peer[d]).wait_recv()
            if early(d, h):
                forward(d, h)
            if h + 1 < own_heads:
                kv_copy(d, h + 1, me).start()
            else:
                q_copy(d, 0, me).start()
    for d in peers:
        w_copy(d, peer[d]).wait_recv()

    def window_of(h, i, low, high):
        return jnp.concatenate(
            [kv[p, h, f, i, c] for p in range(3) for c in range(low, high) for f in range(count)],
            axis=0,
        )

    factor = math.log2(math.e) / math.sqrt(D_HEAD)
    for h in range(own_heads):
        for d in peers:
            q_copy(d, h, peer[d]).wait_recv()
            if h + 1 < own_heads:
                q_copy(d, h + 1, me).start()
        for side in range(2):
            @pl.when(can_take[side])
            def _(side=side):
                for d in range(count):
                    z_copy(side, d, h).wait_recv()
        if h + 1 < own_heads:
            for d in range(count):
                if not early(d, h + 1):
                    forward(d, h + 1)
        for w in range(count):
            low, high = max(w - 1, 0), min(w + 2, count)
            query = qs[h, :, w].reshape(-1, D_HEAD)
            pattern = win[w, 0:1, :]
            wide = high - low
            keys = window_of(h, 0, low, high)
            scores = lax.dot_general(
                query, keys, (((1,), (1,)), ((), ())), preferred_element_type=jnp.float32
            )
            blocks, limits, peak = [], [], None
            for i in range(3 * wide):
                p, c = i // wide, low + i % wide
                start = i * query.shape[0]
                halves = [
                    scores[:, j : j + LANES] for j in range(start, start + query.shape[0], LANES)
                ]
                entry = 9 * p + 3 + (c - w + 1)
                ok = pattern[:, entry : entry + 1] == 1
                if p != 1:
                    ok = jnp.logical_and(ok, can_take[p // 2])
                limit = jnp.where(ok, 0.0, jnp.inf).astype(jnp.float32)
                top = functools.reduce(jnp.maximum, halves) - limit
                peak = top if peak is None else jnp.maximum(peak, top)
                blocks.append(halves)
                limits.append(limit)
            peak = jnp.broadcast_to(jnp.max(peak, axis=1, keepdims=True), peak.shape)
            total, rounded = None, []
            for halves, limit in zip(blocks, limits):
                base = peak + limit
                for half in halves:
                    weights = jnp.exp2((half - base) * factor)
                    total = weights if total is None else total + weights
                    rounded.append(weights.astype(jnp.bfloat16))
            total = jnp.sum(total, axis=1, keepdims=True)
            mixed = jnp.dot(
                jnp.concatenate(rounded, axis=1),
                window_of(h, 1, low, high),
                preferred_element_type=jnp.float32,
            )
            outs[h, w] = (mixed / total).astype(jnp.bfloat16)
            for d in peers:
                o_copy(d, h, w).start()

    for h in range(own_heads):
        out_ref[:, columns_of(me, h)] = by_rows([outs[h, w, rows_of(me)] for w in range(count)])
        for d in peers:
            for w in range(count):
                o_copy(d, h, w).wait_recv()
            out_ref[:, columns_of(peer[d], h)] = by_rows([arrived[d - 1, h, w] for w in range(count)])

    for h in range(own_heads):
        for d in peers:
            kv_copy(d, h, me).wait_send()
            q_copy(d, h, me).wait_send()
            for w in range(count):
                o_copy(d, h, w).wait_send()
        for side in range(2):
            @pl.when(can_send[side])
            def _(side=side):
                for d in range(count):
                    z_copy(side, d, h).wait_send()
    for d in peers:
        w_copy(d, me).wait_send()


def fused(queries, keys, values, window):
    count, times = lax.axis_size("spatial"), lax.axis_size("temporal")
    tokens, channels = queries.shape
    own = channels // (D_HEAD * count)
    part = tokens // count
    vmem = pl.BlockSpec(memory_space=pltpu.VMEM)
    dma = pltpu.SemaphoreType.DMA
    pairs = own * count * (3 * count - 2) * 3 * tokens * tokens * D_HEAD
    return pl.pallas_call(
        functools.partial(fused_kernel, times, count, own),
        out_shape=jax.ShapeDtypeStruct(queries.shape, queries.dtype),
        in_specs=[pl.BlockSpec(memory_space=pl.ANY)] * 4,
        out_specs=vmem,
        scratch_shapes=[
            pltpu.VMEM(queries.shape, jnp.bfloat16),
            pltpu.VMEM(queries.shape, jnp.bfloat16),
            pltpu.VMEM(queries.shape, jnp.bfloat16),
            pltpu.VMEM((1, window.size), jnp.int32),
            pltpu.VMEM((count - 1, own, 2, count, part, D_HEAD), jnp.bfloat16),
            pltpu.VMEM((count - 1, own, count, part, D_HEAD), jnp.bfloat16),
            pltpu.VMEM((3, own, count, 2, count, part, D_HEAD), jnp.bfloat16),
            pltpu.VMEM((own, count, count, part, D_HEAD), jnp.bfloat16),
            pltpu.VMEM((own, count, tokens, D_HEAD), jnp.bfloat16),
            pltpu.VMEM((count - 1, own, count, part, D_HEAD), jnp.bfloat16),
            pltpu.VMEM((count, 8, 128), jnp.int32),
            dma((count - 1, own)), dma((count - 1, own)),
            dma((count - 1, own)), dma((count - 1, own)),
            dma((2, count, own)), dma((2, count, own)),
            dma((count - 1, own, count)), dma((count - 1, own, count)),
            dma((count - 1,)), dma((count - 1,)),
            dma((3, count, own)), dma,
        ],
        compiler_params=pltpu.CompilerParams(
            collective_id=0, has_side_effects=True, vmem_limit_bytes=60 * 2**20
        ),
        cost_estimate=pl.CostEstimate(
            flops=4 * pairs, bytes_accessed=4 * tokens * channels * 2, transcendentals=pairs // D_HEAD
        ),
    )(queries, keys, values, window.reshape(1, -1))


def body(queries, keys, values, window):
    count = lax.axis_size("spatial")
    tokens, channels = queries.shape
    heads_here = channels // D_HEAD
    whole_tiles = window.shape[1] == 1 and window.shape[2] == 1 and tokens == TILE_T * TILE_H * TILE_W
    if whole_tiles and count & (count - 1) == 0 and heads_here % count == 0:
        return fused(queries, keys, values, window)
    return gathered(queries, keys, values, window)


def solution(mesh):
    return jax.shard_map(
        body,
        mesh=mesh,
        in_specs=(
            P(("temporal", "spatial"), "head"),
            P(("temporal", "spatial"), "head"),
            P(("temporal", "spatial"), "head"),
            P("temporal", None, "spatial", None),
        ),
        out_specs=P(("temporal", "spatial"), "head"),
        check_vma=False,
    )
```

```python
import functools
import math

import jax
import jax.numpy as jnp
from jax import lax
from jax.experimental import pallas as pl
from jax.experimental.pallas import tpu as pltpu
from jax.sharding import PartitionSpec as P

D_HEAD = 128
TILE_T = 4
TILE_H = 8
TILE_W = 8
LANES = 128
MESH = pl.DeviceIdType.MESH


def with_halo(array, sides, width):
    for axis, dim in sides:
        peers, length = (lax.axis_size(axis), array.shape[dim])
        up = [(i, (i + 1) % peers) for i in range(peers - 1)]
        down = [(j, i) for i, j in up]
        last = lax.slice_in_dim(array, length - width, length, axis=dim)
        initial = lax.slice_in_dim(array, 0, width, axis=dim)
        before = lax.ppermute(last, axis, up)
        after = lax.ppermute(initial, axis, down)
        array = jnp.concatenate([before, array, after], axis=dim)
    return array


def tile_mask(pattern, tile_row, first_row, window_rows, time_ok, width_ok):
    height_step = first_row - tile_row
    picked = [pattern[:, height_step + 1, :] == 1]
    chosen = jnp.stack(picked, axis=1)
    allowed = chosen & time_ok[:, None, None] & width_ok[None, None, :]
    return jnp.broadcast_to(
        allowed[:, None, :, None, :, None], (3, TILE_T, window_rows, TILE_H, 3, TILE_W)
    ).reshape(-1)


def attend(query_tile, key_window, value_window, key_ok):
    heads_here = query_tile.shape[1]
    group = min(2, heads_here)
    scale = 1.0 / math.sqrt(D_HEAD)
    pieces = []
    for head_start in range(0, heads_here, group):
        query_part = query_tile[:, head_start : head_start + group]
        key_part = key_window[:, head_start : head_start + group]
        value_part = value_window[:, head_start : head_start + group]
        scores = (
            jnp.einsum("qhd,khd->hqk", query_part, key_part, preferred_element_type=jnp.float32)
            * scale
        )
        scores = jnp.where(key_ok[None, None, :], scores, -jnp.inf)
        peak = jnp.max(scores, axis=-1, keepdims=True)
        weights = jnp.exp(scores - peak)
        total = jnp.sum(weights, axis=-1)
        attended_part = jnp.einsum(
            "hqk,khd->qhd",
            weights.astype(jnp.bfloat16),
            value_part,
            preferred_element_type=jnp.float32,
        )
        attended_part = attended_part / jnp.transpose(total)[:, :, None]
        pieces.append(attended_part.astype(jnp.bfloat16).reshape(attended_part.shape[0], -1))
    return jnp.concatenate(pieces, axis=1)


def gathered(queries, keys, values, window):
    space_count = lax.axis_size("spatial")
    time_count = lax.axis_size("temporal")
    tokens_dev, channels = queries.shape
    tile_rows = window.shape[1]
    height = tile_rows * TILE_H
    shard_rows = tokens_dev // (space_count * TILE_W)
    split = 1
    groups = space_count // split
    span = split * TILE_W
    part_channels = channels // split

    def to_blocks(tensor):
        shaped = tensor.reshape(shard_rows, groups, span, split, part_channels)
        return jnp.transpose(shaped, (3, 1, 0, 2, 4)).reshape(
            space_count, shard_rows, span, part_channels
        )

    def from_blocks(tensor):
        return tensor.reshape(TILE_T, height, span, part_channels)

    query_block, key_block, value_block = (
        lax.all_to_all(to_blocks(queries), "spatial", split_axis=0, concat_axis=0, tiled=True),
        lax.all_to_all(to_blocks(keys), "spatial", split_axis=0, concat_axis=0, tiled=True),
        lax.all_to_all(to_blocks(values), "spatial", split_axis=0, concat_axis=0, tiled=True),
    )
    add_key_block = from_blocks(key_block)
    add_value_block = from_blocks(value_block)
    paired = jnp.stack([add_key_block, add_value_block]).reshape(
        2, 1, TILE_T, height, split, TILE_W, part_channels
    )
    padded = with_halo(paired, (("temporal", 1), ("spatial", 4)), 1)
    query_block = from_blocks(query_block)
    column_base = lax.axis_index("spatial")
    offsets = jnp.arange(3, dtype=jnp.int32) - 1
    time_index = lax.axis_index("temporal") + offsets
    time_ok = (time_index >= 0) & (time_index < time_count)
    window_rows = min(3, tile_rows)
    heads_here = part_channels // D_HEAD
    width_index = column_base + 0 + offsets
    width_ok = (width_index >= 0) & (width_index < space_count)
    pattern_column = lax.dynamic_index_in_dim(window, 0, 2, keepdims=False)
    pattern_rows = pattern_column.reshape(tile_rows, 3, 3, 3)
    first_row = min(max(0 - 1, 0), tile_rows - window_rows)
    key_ok = tile_mask(pattern_rows[0], 0, first_row, window_rows, time_ok, width_ok)
    query_tile = query_block.reshape(-1, heads_here, D_HEAD)
    row_low = first_row * TILE_H
    row_high = row_low + window_rows * TILE_H
    key_window = padded[0, :, :, row_low:row_high, 0:3].reshape(-1, heads_here, D_HEAD)
    value_window = padded[1, :, :, row_low:row_high, 0:3].reshape(-1, heads_here, D_HEAD)
    attended_tile = attend(query_tile, key_window, value_window, key_ok)
    outputs = attended_tile.reshape(TILE_T, TILE_H, TILE_W, part_channels)
    result = outputs.reshape(space_count, shard_rows, span, part_channels)
    returned = lax.all_to_all(result, "spatial", split_axis=0, concat_axis=0, tiled=True)
    shaped = returned.reshape(split, groups, shard_rows, span, part_channels)
    return jnp.transpose(shaped, (2, 1, 3, 0, 4)).reshape(tokens_dev, channels)


def flipped(index, bits):
    bit = 1
    while bit <= bits:
        if bits & bit:
            index = index + bit - 2 * bit * ((index // bit) % 2)
        bit *= 2
    return index


def by_tiles(rows, count):
    width = count * TILE_W
    whole = rows.astype(jnp.float32)
    lines = whole.shape[0] // width
    return [
        jnp.concatenate(
            [whole[r * width + w * TILE_W : r * width + (w + 1) * TILE_W] for r in range(lines)],
            axis=0,
        ).astype(rows.dtype)
        for w in range(count)
    ]


def by_rows(parts):
    parts = [part.astype(jnp.float32) for part in parts]
    lines = parts[0].shape[0] // TILE_W
    return jnp.concatenate(
        [part[r * TILE_W : (r + 1) * TILE_W] for r in range(lines) for part in parts], axis=0
    ).astype(jnp.bfloat16)


def fused_kernel(
    times, count, own_heads,
    q_hbm, k_hbm, v_hbm, win_hbm, out_ref,
    q_ref, k_ref, v_ref, win_ref, stage_kv, stage_q, kv, qs, outs, arrived, win,
    kv_send, kv_recv, q_send, q_recv, z_send, z_recv, o_send, o_recv, w_send, w_recv,
    in_sem, win_sem,
):
    t = lax.axis_index("temporal")
    me = lax.axis_index("spatial")
    part = q_ref.shape[0] // count
    peers = range(1, count)
    peer = [flipped(me, d) for d in range(count)]

    def columns_of(index, h):
        return pl.ds(pl.multiple_of((index * own_heads + h) * D_HEAD, D_HEAD), D_HEAD)

    def to(d):
        return {"spatial": peer[d]}

    def kv_copy(d, h, shard):
        return pltpu.make_async_remote_copy(
            src_ref=stage_kv.at[d - 1, h],
            dst_ref=kv.at[1, h, shard],
            send_sem=kv_send.at[d - 1, h],
            recv_sem=kv_recv.at[d - 1, h],
            device_id=to(d), device_id_type=MESH,
        )

    def q_copy(d, h, shard):
        return pltpu.make_async_remote_copy(
            src_ref=stage_q.at[d - 1, h],
            dst_ref=qs.at[h, shard],
            send_sem=q_send.at[d - 1, h],
            recv_sem=q_recv.at[d - 1, h],
            device_id=to(d), device_id_type=MESH,
        )

    def w_copy(d, slot):
        return pltpu.make_async_remote_copy(
            src_ref=win.at[slot],
            dst_ref=win.at[slot],
            send_sem=w_send.at[d - 1],
            recv_sem=w_recv.at[d - 1],
            device_id=to(d), device_id_type=MESH,
        )

    def z_copy(side, d, h):
        return pltpu.make_async_remote_copy(
            src_ref=kv.at[1, h, peer[d]],
            dst_ref=kv.at[2 * side, h, peer[d]],
            send_sem=z_send.at[side, d, h],
            recv_sem=z_recv.at[side, d, h],
            device_id={"temporal": t + 1 - 2 * side}, device_id_type=MESH,
        )

    def o_parts(h):
        half = max(count // 2, 1)
        return [(0, count)] if h + 1 < own_heads or half == count else [(0, half), (half, count - half)]

    def o_copy(d, h, j):
        tiles = pl.ds(*o_parts(h)[j])
        return pltpu.make_async_remote_copy(
            src_ref=outs.at[h, peer[d], tiles],
            dst_ref=arrived.at[d - 1, h, tiles],
            send_sem=o_send.at[d - 1, h, j],
            recv_sem=o_recv.at[d - 1, h, j],
            device_id=to(d), device_id_type=MESH,
        )

    def in_copy(i, d):
        wide = own_heads * D_HEAD
        here = pl.ds(pl.multiple_of(peer[d] * wide, wide), wide)
        return pltpu.make_async_copy(
            (k_hbm, v_hbm)[i].at[:, here], (k_ref, v_ref)[i].at[:, here], in_sem.at[i, d]
        )

    for d in range(count):
        for i in range(2):
            in_copy(i, d).start()
    win_copy = pltpu.make_async_copy(win_hbm, win_ref, win_sem.at[0])
    win_copy.start()
    q_in = pltpu.make_async_copy(q_hbm, q_ref, win_sem.at[1])
    q_in.start()

    can_send = (t < times - 1, t > 0)
    can_take = (t > 0, t < times - 1)

    barrier = pltpu.get_barrier_semaphore()
    for d in peers:
        pl.semaphore_signal(barrier, inc=1, device_id=to(d), device_id_type=MESH)
    for side in range(2):
        @pl.when(can_send[side])
        def _(side=side):
            pl.semaphore_signal(
                barrier, inc=1, device_id={"temporal": t + 1 - 2 * side}, device_id_type=MESH
            )

    def lay_kv(d, h):
        for i, ref in enumerate((k_ref, v_ref)):
            if h == 0:
                in_copy(i, d).wait()
            for w, piece in enumerate(by_tiles(ref[:, columns_of(peer[d], h)], count)):
                if d:
                    stage_kv[d - 1, h, i, w] = piece
                else:
                    kv[1, h, me, i, w] = piece

    def lay_q(d, h):
        if d == 0 and h == 0:
            q_in.wait()
        for w, piece in enumerate(by_tiles(q_ref[:, columns_of(peer[d], h)], count)):
            if d:
                stage_q[d - 1, h, w] = piece
            else:
                qs[h, me, w] = piece

    def forward(d, h):
        for side in range(2):
            @pl.when(can_send[side])
            def _(side=side):
                z_copy(side, d, h).start()

    lay_kv(0, 0)
    win_copy.wait()
    win[me] = jnp.zeros(win.shape[1:], win.dtype)
    win[me, 0:1, 0 : win_ref.shape[1]] = win_ref[...]
    for side in range(2):
        @pl.when(jnp.logical_not(can_take[side]))
        def _(side=side):
            kv[2 * side] = jnp.zeros(kv.shape[1:], kv.dtype)

    linked = can_send[0].astype(jnp.int32) + can_send[1].astype(jnp.int32)
    pl.semaphore_wait(barrier, count - 1 + linked)

    def early(d, h):
        return h == 0 or (h == 1 and d <= 1)

    forward(0, 0)
    for d in peers:
        lay_kv(d, 0)
        kv_copy(d, 0, me).start()
    for d in peers:
        w_copy(d, me).start()
    for h in range(1, own_heads):
        for d in range(count):
            lay_kv(d, h)
            if d == 0 and early(d, h):
                forward(d, h)
    for h in range(own_heads):
        for d in range(count):
            lay_q(d, h)

    for h in range(own_heads):
        for d in peers:
            kv_copy(d, h, peer[d]).wait_recv()
            if early(d, h):
                forward(d, h)
            if h + 1 < own_heads:
                kv_copy(d, h + 1, me).start()
            else:
                q_copy(d, 0, me).start()
    for d in peers:
        w_copy(d, peer[d]).wait_recv()

    def bring_home(h):
        out_ref[:, columns_of(me, h)] = by_rows([outs[h, me, w] for w in range(count)])
        for d in peers:
            for j in range(len(o_parts(h))):
                o_copy(d, h, j).wait_recv()
            out_ref[:, columns_of(peer[d], h)] = by_rows([arrived[d - 1, h, w] for w in range(count)])

    def window_of(h, i, low, high):
        return jnp.concatenate(
            [kv[p, h, f, i, c] for p in range(3) for c in range(low, high) for f in range(count)],
            axis=0,
        )

    factor = math.log2(math.e) / math.sqrt(D_HEAD)
    for h in range(own_heads):
        for d in peers:
            q_copy(d, h, peer[d]).wait_recv()
            if h + 1 < own_heads:
                q_copy(d, h + 1, me).start()
        if h:
            bring_home(h - 1)
        for side in range(2):
            @pl.when(can_take[side])
            def _(side=side):
                for d in range(count):
                    z_copy(side, d, h).wait_recv()
        if h + 1 < own_heads:
            for d in range(count):
                if not early(d, h + 1):
                    forward(d, h + 1)
        for w in range(count):
            low, high = max(w - 1, 0), min(w + 2, count)
            query = qs[h, :, w].reshape(-1, D_HEAD)
            pattern = win[w, 0:1, :]
            wide = high - low
            keys = window_of(h, 0, low, high)
            scores = lax.dot_general(
                query, keys, (((1,), (1,)), ((), ())), preferred_element_type=jnp.float32
            )
            blocks, limits, peak = [], [], None
            for i in range(3 * wide):
                p, c = i // wide, low + i % wide
                start = i * query.shape[0]
                halves = [
                    scores[:, j : j + LANES] for j in range(start, start + query.shape[0], LANES)
                ]
                entry = 9 * p + 3 + (c - w + 1)
                ok = pattern[:, entry : entry + 1] == 1
                if p != 1:
                    ok = jnp.logical_and(ok, can_take[p // 2])
                limit = jnp.where(ok, 0.0, jnp.inf).astype(jnp.float32)
                top = functools.reduce(jnp.maximum, halves) - limit
                peak = top if peak is None else jnp.maximum(peak, top)
                blocks.append(halves)
                limits.append(limit)
            peak = jnp.broadcast_to(jnp.max(peak, axis=1, keepdims=True), peak.shape)
            total, rounded = None, []
            for halves, limit in zip(blocks, limits):
                base = peak + limit
                for half in halves:
                    weights = jnp.exp2((half - base) * factor)
                    total = weights if total is None else total + weights
                    rounded.append(weights.astype(jnp.bfloat16))
            total = jnp.sum(total, axis=1, keepdims=True)
            mixed = jnp.dot(
                jnp.concatenate(rounded, axis=1),
                window_of(h, 1, low, high),
                preferred_element_type=jnp.float32,
            )
            attended = (mixed / total).astype(jnp.bfloat16)
            for f in range(count):
                outs[h, f, w] = attended[f * part : (f + 1) * part]
            for j, (first, number) in enumerate(o_parts(h)):
                if w == first + number - 1:
                    for d in peers:
                        o_copy(d, h, j).start()

    bring_home(own_heads - 1)

    for h in range(own_heads):
        for d in peers:
            kv_copy(d, h, me).wait_send()
            q_copy(d, h, me).wait_send()
            for j in range(len(o_parts(h))):
                o_copy(d, h, j).wait_send()
        for side in range(2):
            @pl.when(can_send[side])
            def _(side=side):
                for d in range(count):
                    z_copy(side, d, h).wait_send()
    for d in peers:
        w_copy(d, me).wait_send()


def fused(queries, keys, values, window):
    count, times = lax.axis_size("spatial"), lax.axis_size("temporal")
    tokens, channels = queries.shape
    own = channels // (D_HEAD * count)
    part = tokens // count
    vmem = pl.BlockSpec(memory_space=pltpu.VMEM)
    dma = pltpu.SemaphoreType.DMA
    pairs = own * count * (3 * count - 2) * 3 * tokens * tokens * D_HEAD
    return pl.pallas_call(
        functools.partial(fused_kernel, times, count, own),
        out_shape=jax.ShapeDtypeStruct(queries.shape, queries.dtype),
        in_specs=[pl.BlockSpec(memory_space=pl.ANY)] * 4,
        out_specs=vmem,
        scratch_shapes=[
            pltpu.VMEM(queries.shape, jnp.bfloat16),
            pltpu.VMEM(queries.shape, jnp.bfloat16),
            pltpu.VMEM(queries.shape, jnp.bfloat16),
            pltpu.VMEM((1, window.size), jnp.int32),
            pltpu.VMEM((count - 1, own, 2, count, part, D_HEAD), jnp.bfloat16),
            pltpu.VMEM((count - 1, own, count, part, D_HEAD), jnp.bfloat16),
            pltpu.VMEM((3, own, count, 2, count, part, D_HEAD), jnp.bfloat16),
            pltpu.VMEM((own, count, count, part, D_HEAD), jnp.bfloat16),
            pltpu.VMEM((own, count, count, part, D_HEAD), jnp.bfloat16),
            pltpu.VMEM((count - 1, own, count, part, D_HEAD), jnp.bfloat16),
            pltpu.VMEM((count, 8, 128), jnp.int32),
            dma((count - 1, own)), dma((count - 1, own)),
            dma((count - 1, own)), dma((count - 1, own)),
            dma((2, count, own)), dma((2, count, own)),
            dma((count - 1, own, 2)), dma((count - 1, own, 2)),
            dma((count - 1,)), dma((count - 1,)),
            dma((2, count)), dma((2,)),
        ],
        compiler_params=pltpu.CompilerParams(
            collective_id=0, has_side_effects=True, vmem_limit_bytes=60 * 2**20
        ),
        cost_estimate=pl.CostEstimate(
            flops=4 * pairs, bytes_accessed=4 * tokens * channels * 2, transcendentals=pairs // D_HEAD
        ),
    )(queries, keys, values, window.reshape(1, -1))


def body(queries, keys, values, window):
    count = lax.axis_size("spatial")
    tokens, channels = queries.shape
    heads_here = channels // D_HEAD
    whole_tiles = window.shape[1] == 1 and window.shape[2] == 1 and tokens == TILE_T * TILE_H * TILE_W
    if whole_tiles and count & (count - 1) == 0 and heads_here % count == 0:
        return fused(queries, keys, values, window)
    return gathered(queries, keys, values, window)


def solution(mesh):
    return jax.shard_map(
        body,
        mesh=mesh,
        in_specs=(
            P(("temporal", "spatial"), "head"),
            P(("temporal", "spatial"), "head"),
            P(("temporal", "spatial"), "head"),
            P("temporal", None, "spatial", None),
        ),
        out_specs=P(("temporal", "spatial"), "head"),
        check_vma=False,
    )
```

```python
import functools
import math

import jax
import jax.numpy as jnp
from jax import lax
from jax.experimental import pallas as pl
from jax.experimental.pallas import tpu as pltpu
from jax.sharding import PartitionSpec as P

D_HEAD = 128
TILE_T = 4
TILE_H = 8
TILE_W = 8
LANES = 128
MESH = pl.DeviceIdType.MESH


def with_halo(array, sides, width):
    for axis, dim in sides:
        peers, length = (lax.axis_size(axis), array.shape[dim])
        up = [(i, (i + 1) % peers) for i in range(peers - 1)]
        down = [(j, i) for i, j in up]
        last = lax.slice_in_dim(array, length - width, length, axis=dim)
        initial = lax.slice_in_dim(array, 0, width, axis=dim)
        before = lax.ppermute(last, axis, up)
        after = lax.ppermute(initial, axis, down)
        array = jnp.concatenate([before, array, after], axis=dim)
    return array


def tile_mask(pattern, tile_row, first_row, window_rows, time_ok, width_ok):
    height_step = first_row - tile_row
    picked = [pattern[:, height_step + 1, :] == 1]
    chosen = jnp.stack(picked, axis=1)
    allowed = chosen & time_ok[:, None, None] & width_ok[None, None, :]
    return jnp.broadcast_to(
        allowed[:, None, :, None, :, None], (3, TILE_T, window_rows, TILE_H, 3, TILE_W)
    ).reshape(-1)


def attend(query_tile, key_window, value_window, key_ok):
    heads_here = query_tile.shape[1]
    group = min(2, heads_here)
    scale = 1.0 / math.sqrt(D_HEAD)
    pieces = []
    for head_start in range(0, heads_here, group):
        query_part = query_tile[:, head_start : head_start + group]
        key_part = key_window[:, head_start : head_start + group]
        value_part = value_window[:, head_start : head_start + group]
        scores = (
            jnp.einsum("qhd,khd->hqk", query_part, key_part, preferred_element_type=jnp.float32)
            * scale
        )
        scores = jnp.where(key_ok[None, None, :], scores, -jnp.inf)
        peak = jnp.max(scores, axis=-1, keepdims=True)
        weights = jnp.exp(scores - peak)
        total = jnp.sum(weights, axis=-1)
        attended_part = jnp.einsum(
            "hqk,khd->qhd",
            weights.astype(jnp.bfloat16),
            value_part,
            preferred_element_type=jnp.float32,
        )
        attended_part = attended_part / jnp.transpose(total)[:, :, None]
        pieces.append(attended_part.astype(jnp.bfloat16).reshape(attended_part.shape[0], -1))
    return jnp.concatenate(pieces, axis=1)


def gathered(queries, keys, values, window):
    space_count = lax.axis_size("spatial")
    time_count = lax.axis_size("temporal")
    tokens_dev, channels = queries.shape
    tile_rows = window.shape[1]
    height = tile_rows * TILE_H
    shard_rows = tokens_dev // (space_count * TILE_W)
    split = 1
    groups = space_count // split
    span = split * TILE_W
    part_channels = channels // split

    def to_blocks(tensor):
        shaped = tensor.reshape(shard_rows, groups, span, split, part_channels)
        return jnp.transpose(shaped, (3, 1, 0, 2, 4)).reshape(
            space_count, shard_rows, span, part_channels
        )

    def from_blocks(tensor):
        return tensor.reshape(TILE_T, height, span, part_channels)

    query_block, key_block, value_block = (
        lax.all_to_all(to_blocks(queries), "spatial", split_axis=0, concat_axis=0, tiled=True),
        lax.all_to_all(to_blocks(keys), "spatial", split_axis=0, concat_axis=0, tiled=True),
        lax.all_to_all(to_blocks(values), "spatial", split_axis=0, concat_axis=0, tiled=True),
    )
    add_key_block = from_blocks(key_block)
    add_value_block = from_blocks(value_block)
    paired = jnp.stack([add_key_block, add_value_block]).reshape(
        2, 1, TILE_T, height, split, TILE_W, part_channels
    )
    padded = with_halo(paired, (("temporal", 1), ("spatial", 4)), 1)
    query_block = from_blocks(query_block)
    column_base = lax.axis_index("spatial")
    offsets = jnp.arange(3, dtype=jnp.int32) - 1
    time_index = lax.axis_index("temporal") + offsets
    time_ok = (time_index >= 0) & (time_index < time_count)
    window_rows = min(3, tile_rows)
    heads_here = part_channels // D_HEAD
    width_index = column_base + 0 + offsets
    width_ok = (width_index >= 0) & (width_index < space_count)
    pattern_column = lax.dynamic_index_in_dim(window, 0, 2, keepdims=False)
    pattern_rows = pattern_column.reshape(tile_rows, 3, 3, 3)
    first_row = min(max(0 - 1, 0), tile_rows - window_rows)
    key_ok = tile_mask(pattern_rows[0], 0, first_row, window_rows, time_ok, width_ok)
    query_tile = query_block.reshape(-1, heads_here, D_HEAD)
    row_low = first_row * TILE_H
    row_high = row_low + window_rows * TILE_H
    key_window = padded[0, :, :, row_low:row_high, 0:3].reshape(-1, heads_here, D_HEAD)
    value_window = padded[1, :, :, row_low:row_high, 0:3].reshape(-1, heads_here, D_HEAD)
    attended_tile = attend(query_tile, key_window, value_window, key_ok)
    outputs = attended_tile.reshape(TILE_T, TILE_H, TILE_W, part_channels)
    result = outputs.reshape(space_count, shard_rows, span, part_channels)
    returned = lax.all_to_all(result, "spatial", split_axis=0, concat_axis=0, tiled=True)
    shaped = returned.reshape(split, groups, shard_rows, span, part_channels)
    return jnp.transpose(shaped, (2, 1, 3, 0, 4)).reshape(tokens_dev, channels)


def flipped(index, bits):
    bit = 1
    while bit <= bits:
        if bits & bit:
            index = index + bit - 2 * bit * ((index // bit) % 2)
        bit *= 2
    return index


def by_tiles(rows, count):
    width = count * TILE_W
    whole = rows.astype(jnp.float32)
    lines = whole.shape[0] // width
    return [
        jnp.concatenate(
            [whole[r * width + w * TILE_W : r * width + (w + 1) * TILE_W] for r in range(lines)],
            axis=0,
        ).astype(rows.dtype)
        for w in range(count)
    ]


def by_rows(parts):
    parts = [part.astype(jnp.float32) for part in parts]
    lines = parts[0].shape[0] // TILE_W
    return jnp.concatenate(
        [part[r * TILE_W : (r + 1) * TILE_W] for r in range(lines) for part in parts], axis=0
    ).astype(jnp.bfloat16)


def column_groups(count):
    first = min(2, count)
    return [(0, first)] + [(c, 1) for c in range(first, count)]


def fused_kernel(
    times, count, own_heads,
    q_hbm, k_hbm, v_hbm, win_hbm, out_ref,
    q_ref, k_ref, v_ref, win_ref, stage_kv, stage_q, kv, qs, outs, arrived, win,
    kv_send, kv_recv, q_send, q_recv, z_send, z_recv, o_send, o_recv, w_send, w_recv,
    in_sem, win_sem,
):
    t = lax.axis_index("temporal")
    me = lax.axis_index("spatial")
    part = q_ref.shape[0] // count
    peers = range(1, count)
    peer = [flipped(me, d) for d in range(count)]

    def rows_of(index):
        return pl.ds(pl.multiple_of(index * part, part), part)

    def columns_of(index, h):
        return pl.ds(pl.multiple_of((index * own_heads + h) * D_HEAD, D_HEAD), D_HEAD)

    def to(d):
        return {"spatial": peer[d]}

    def kv_copy(d, h, shard):
        return pltpu.make_async_remote_copy(
            src_ref=stage_kv.at[d - 1, h],
            dst_ref=kv.at[1, h, shard],
            send_sem=kv_send.at[d - 1, h],
            recv_sem=kv_recv.at[d - 1, h],
            device_id=to(d), device_id_type=MESH,
        )

    def q_copy(d, h, shard):
        return pltpu.make_async_remote_copy(
            src_ref=stage_q.at[d - 1, h],
            dst_ref=qs.at[h, shard],
            send_sem=q_send.at[d - 1, h],
            recv_sem=q_recv.at[d - 1, h],
            device_id=to(d), device_id_type=MESH,
        )

    def w_copy(d, slot):
        return pltpu.make_async_remote_copy(
            src_ref=win.at[slot],
            dst_ref=win.at[slot],
            send_sem=w_send.at[d - 1],
            recv_sem=w_recv.at[d - 1],
            device_id=to(d), device_id_type=MESH,
        )

    def groups(h):
        return column_groups(count) if h + 1 == own_heads else [(0, count)]

    def z_copy(side, d, h, j):
        tiles = pl.ds(*groups(h)[j])
        return pltpu.make_async_remote_copy(
            src_ref=kv.at[1, h, peer[d], :, tiles],
            dst_ref=kv.at[2 * side, h, peer[d], :, tiles],
            send_sem=z_send.at[side, d, h, j],
            recv_sem=z_recv.at[side, d, h, j],
            device_id={"temporal": t + 1 - 2 * side}, device_id_type=MESH,
        )

    def o_copy(d, h, w):
        return pltpu.make_async_remote_copy(
            src_ref=outs.at[h, w, rows_of(peer[d])],
            dst_ref=arrived.at[d - 1, h, w],
            send_sem=o_send.at[d - 1, h, w],
            recv_sem=o_recv.at[d - 1, h, w],
            device_id=to(d), device_id_type=MESH,
        )

    def in_copy(i, d, h):
        here = columns_of(peer[d], h)
        return pltpu.make_async_copy(
            (k_hbm, v_hbm, q_hbm)[i].at[:, here],
            (k_ref, v_ref, q_ref)[i].at[:, here],
            in_sem.at[i, d, h],
        )

    for h in range(own_heads):
        for d in range(count):
            for i in range(2):
                in_copy(i, d, h).start()
    win_copy = pltpu.make_async_copy(win_hbm, win_ref, win_sem)
    win_copy.start()
    for h in range(own_heads):
        for d in range(count):
            in_copy(2, d, h).start()

    can_send = (t < times - 1, t > 0)
    can_take = (t > 0, t < times - 1)

    barrier = pltpu.get_barrier_semaphore()
    for d in peers:
        pl.semaphore_signal(barrier, inc=1, device_id=to(d), device_id_type=MESH)
    for side in range(2):
        @pl.when(can_send[side])
        def _(side=side):
            pl.semaphore_signal(
                barrier, inc=1, device_id={"temporal": t + 1 - 2 * side}, device_id_type=MESH
            )

    def lay_kv(d, h):
        for i, ref in enumerate((k_ref, v_ref)):
            in_copy(i, d, h).wait()
            for w, piece in enumerate(by_tiles(ref[:, columns_of(peer[d], h)], count)):
                if d:
                    stage_kv[d - 1, h, i, w] = piece
                else:
                    kv[1, h, me, i, w] = piece

    def lay_q(d, h):
        in_copy(2, d, h).wait()
        for w, piece in enumerate(by_tiles(q_ref[:, columns_of(peer[d], h)], count)):
            if d:
                stage_q[d - 1, h, w] = piece
            else:
                qs[h, me, w] = piece

    def forward(d, h, some=slice(None)):
        for side in range(2):
            @pl.when(can_send[side])
            def _(side=side):
                for j in range(len(groups(h)))[some]:
                    z_copy(side, d, h, j).start()

    def forward_late(h, some):
        for d in range(count):
            if h < own_heads and not early(d, h):
                forward(d, h, some)

    def take(h, some=slice(None)):
        for side in range(2):
            @pl.when(can_take[side])
            def _(side=side):
                for j in range(len(groups(h)))[some]:
                    for d in range(count):
                        z_copy(side, d, h, j).wait_recv()

    lay_kv(0, 0)
    win_copy.wait()
    win[me] = jnp.zeros(win.shape[1:], win.dtype)
    win[me, 0:1, 0 : win_ref.shape[1]] = win_ref[...]
    for side in range(2):
        @pl.when(jnp.logical_not(can_take[side]))
        def _(side=side):
            kv[2 * side] = jnp.zeros(kv.shape[1:], kv.dtype)

    linked = can_send[0].astype(jnp.int32) + can_send[1].astype(jnp.int32)
    pl.semaphore_wait(barrier, count - 1 + linked)

    def early(d, h):
        return h == 0 or (h == 1 and d <= 1)

    forward(0, 0)
    for d in peers:
        lay_kv(d, 0)
        kv_copy(d, 0, me).start()
    for d in peers:
        w_copy(d, me).start()
    for h in range(1, own_heads):
        for d in range(count):
            lay_kv(d, h)
            if d == 0 and early(d, h):
                forward(d, h)
    for h in range(own_heads):
        for d in range(count):
            lay_q(d, h)

    for h in range(own_heads):
        for d in peers:
            kv_copy(d, h, peer[d]).wait_recv()
            if early(d, h):
                forward(d, h)
            if h + 1 < own_heads:
                kv_copy(d, h + 1, me).start()
            else:
                q_copy(d, 0, me).start()
    for d in peers:
        w_copy(d, peer[d]).wait_recv()

    def bring_home(h):
        out_ref[:, columns_of(me, h)] = by_rows([outs[h, w, rows_of(me)] for w in range(count)])
        for d in peers:
            for w in range(count):
                o_copy(d, h, w).wait_recv()
            out_ref[:, columns_of(peer[d], h)] = by_rows([arrived[d - 1, h, w] for w in range(count)])

    def window_of(h, i, low, high):
        return jnp.concatenate(
            [kv[p, h, f, i, c] for p in range(3) for c in range(low, high) for f in range(count)],
            axis=0,
        )

    factor = math.log2(math.e) / math.sqrt(D_HEAD)
    for h in range(own_heads):
        for d in peers:
            q_copy(d, h, peer[d]).wait_recv()
            if h + 1 < own_heads:
                q_copy(d, h + 1, me).start()
        last = h + 1 == own_heads
        if not last:
            take(h)
            forward_late(h + 1, slice(0, 2))
        for w in range(count):
            if last and w < len(groups(h)):
                if w + 1 == len(groups(h)) and h:
                    bring_home(h - 1)
                take(h, slice(w, w + 1))
            if not last and w == count // 2:
                forward_late(h + 1, slice(2, None))
            low, high = max(w - 1, 0), min(w + 2, count)
            query = qs[h, :, w].reshape(-1, D_HEAD)
            pattern = win[w, 0:1, :]
            wide = high - low
            keys = window_of(h, 0, low, high)
            scores = lax.dot_general(
                query, keys, (((1,), (1,)), ((), ())), preferred_element_type=jnp.float32
            )
            blocks, limits, peak = [], [], None
            for i in range(3 * wide):
                p, c = i // wide, low + i % wide
                start = i * query.shape[0]
                halves = [
                    scores[:, j : j + LANES] for j in range(start, start + query.shape[0], LANES)
                ]
                entry = 9 * p + 3 + (c - w + 1)
                ok = pattern[:, entry : entry + 1] == 1
                if p != 1:
                    ok = jnp.logical_and(ok, can_take[p // 2])
                limit = jnp.where(ok, 0.0, jnp.inf).astype(jnp.float32)
                top = functools.reduce(jnp.maximum, halves) - limit
                peak = top if peak is None else jnp.maximum(peak, top)
                blocks.append(halves)
                limits.append(limit)
            peak = jnp.broadcast_to(jnp.max(peak, axis=1, keepdims=True), peak.shape)
            total, rounded = None, []
            for halves, limit in zip(blocks, limits):
                base = peak + limit
                for half in halves:
                    weights = jnp.exp2((half - base) * factor)
                    total = weights if total is None else total + weights
                    rounded.append(weights.astype(jnp.bfloat16))
            total = jnp.sum(total, axis=1, keepdims=True)
            mixed = jnp.dot(
                jnp.concatenate(rounded, axis=1),
                window_of(h, 1, low, high),
                preferred_element_type=jnp.float32,
            )
            outs[h, w] = (mixed / total).astype(jnp.bfloat16)
            for d in peers:
                o_copy(d, h, w).start()

    bring_home(own_heads - 1)

    for h in range(own_heads):
        for d in peers:
            kv_copy(d, h, me).wait_send()
            q_copy(d, h, me).wait_send()
            for w in range(count):
                o_copy(d, h, w).wait_send()
        for side in range(2):
            @pl.when(can_send[side])
            def _(side=side):
                for d in range(count):
                    for j in range(len(groups(h))):
                        z_copy(side, d, h, j).wait_send()
    for d in peers:
        w_copy(d, me).wait_send()


def fused(queries, keys, values, window):
    count, times = lax.axis_size("spatial"), lax.axis_size("temporal")
    tokens, channels = queries.shape
    own = channels // (D_HEAD * count)
    part = tokens // count
    groups = len(column_groups(count))
    vmem = pl.BlockSpec(memory_space=pltpu.VMEM)
    dma = pltpu.SemaphoreType.DMA
    pairs = own * count * (3 * count - 2) * 3 * tokens * tokens * D_HEAD
    return pl.pallas_call(
        functools.partial(fused_kernel, times, count, own),
        out_shape=jax.ShapeDtypeStruct(queries.shape, queries.dtype),
        in_specs=[pl.BlockSpec(memory_space=pl.ANY)] * 4,
        out_specs=vmem,
        scratch_shapes=[
            pltpu.VMEM(queries.shape, jnp.bfloat16),
            pltpu.VMEM(queries.shape, jnp.bfloat16),
            pltpu.VMEM(queries.shape, jnp.bfloat16),
            pltpu.VMEM((1, window.size), jnp.int32),
            pltpu.VMEM((count - 1, own, 2, count, part, D_HEAD), jnp.bfloat16),
            pltpu.VMEM((count - 1, own, count, part, D_HEAD), jnp.bfloat16),
            pltpu.VMEM((3, own, count, 2, count, part, D_HEAD), jnp.bfloat16),
            pltpu.VMEM((own, count, count, part, D_HEAD), jnp.bfloat16),
            pltpu.VMEM((own, count, tokens, D_HEAD), jnp.bfloat16),
            pltpu.VMEM((count - 1, own, count, part, D_HEAD), jnp.bfloat16),
            pltpu.VMEM((count, 8, 128), jnp.int32),
            dma((count - 1, own)), dma((count - 1, own)),
            dma((count - 1, own)), dma((count - 1, own)),
            dma((2, count, own, groups)), dma((2, count, own, groups)),
            dma((count - 1, own, count)), dma((count - 1, own, count)),
            dma((count - 1,)), dma((count - 1,)),
            dma((3, count, own)), dma,
        ],
        compiler_params=pltpu.CompilerParams(
            collective_id=0, has_side_effects=True, vmem_limit_bytes=60 * 2**20
        ),
        cost_estimate=pl.CostEstimate(
            flops=4 * pairs, bytes_accessed=4 * tokens * channels * 2, transcendentals=pairs // D_HEAD
        ),
    )(queries, keys, values, window.reshape(1, -1))


def body(queries, keys, values, window):
    count = lax.axis_size("spatial")
    tokens, channels = queries.shape
    heads_here = channels // D_HEAD
    whole_tiles = window.shape[1] == 1 and window.shape[2] == 1 and tokens == TILE_T * TILE_H * TILE_W
    if whole_tiles and count & (count - 1) == 0 and heads_here % count == 0:
        return fused(queries, keys, values, window)
    return gathered(queries, keys, values, window)


def solution(mesh):
    return jax.shard_map(
        body,
        mesh=mesh,
        in_specs=(
            P(("temporal", "spatial"), "head"),
            P(("temporal", "spatial"), "head"),
            P(("temporal", "spatial"), "head"),
            P("temporal", None, "spatial", None),
        ),
        out_specs=P(("temporal", "spatial"), "head"),
        check_vma=False,
    )
```

```python
import functools
import math

import jax
import jax.numpy as jnp
from jax import lax
from jax.experimental import pallas as pl
from jax.experimental.pallas import tpu as pltpu
from jax.sharding import PartitionSpec as P

D_HEAD = 128
TILE_T = 4
TILE_H = 8
TILE_W = 8
LANES = 128
MESH = pl.DeviceIdType.MESH


def with_halo(array, sides, width):
    for axis, dim in sides:
        peers, length = (lax.axis_size(axis), array.shape[dim])
        up = [(i, (i + 1) % peers) for i in range(peers - 1)]
        down = [(j, i) for i, j in up]
        last = lax.slice_in_dim(array, length - width, length, axis=dim)
        initial = lax.slice_in_dim(array, 0, width, axis=dim)
        before = lax.ppermute(last, axis, up)
        after = lax.ppermute(initial, axis, down)
        array = jnp.concatenate([before, array, after], axis=dim)
    return array


def tile_mask(pattern, tile_row, first_row, window_rows, time_ok, width_ok):
    height_step = first_row - tile_row
    picked = [pattern[:, height_step + 1, :] == 1]
    chosen = jnp.stack(picked, axis=1)
    allowed = chosen & time_ok[:, None, None] & width_ok[None, None, :]
    return jnp.broadcast_to(
        allowed[:, None, :, None, :, None], (3, TILE_T, window_rows, TILE_H, 3, TILE_W)
    ).reshape(-1)


def attend(query_tile, key_window, value_window, key_ok):
    heads_here = query_tile.shape[1]
    group = min(2, heads_here)
    scale = 1.0 / math.sqrt(D_HEAD)
    pieces = []
    for head_start in range(0, heads_here, group):
        query_part = query_tile[:, head_start : head_start + group]
        key_part = key_window[:, head_start : head_start + group]
        value_part = value_window[:, head_start : head_start + group]
        scores = (
            jnp.einsum("qhd,khd->hqk", query_part, key_part, preferred_element_type=jnp.float32)
            * scale
        )
        scores = jnp.where(key_ok[None, None, :], scores, -jnp.inf)
        peak = jnp.max(scores, axis=-1, keepdims=True)
        weights = jnp.exp(scores - peak)
        total = jnp.sum(weights, axis=-1)
        attended_part = jnp.einsum(
            "hqk,khd->qhd",
            weights.astype(jnp.bfloat16),
            value_part,
            preferred_element_type=jnp.float32,
        )
        attended_part = attended_part / jnp.transpose(total)[:, :, None]
        pieces.append(attended_part.astype(jnp.bfloat16).reshape(attended_part.shape[0], -1))
    return jnp.concatenate(pieces, axis=1)


def gathered(queries, keys, values, window):
    space_count = lax.axis_size("spatial")
    time_count = lax.axis_size("temporal")
    tokens_dev, channels = queries.shape
    tile_rows = window.shape[1]
    height = tile_rows * TILE_H
    shard_rows = tokens_dev // (space_count * TILE_W)
    split = 1
    groups = space_count // split
    span = split * TILE_W
    part_channels = channels // split

    def to_blocks(tensor):
        shaped = tensor.reshape(shard_rows, groups, span, split, part_channels)
        return jnp.transpose(shaped, (3, 1, 0, 2, 4)).reshape(
            space_count, shard_rows, span, part_channels
        )

    def from_blocks(tensor):
        return tensor.reshape(TILE_T, height, span, part_channels)

    query_block, key_block, value_block = (
        lax.all_to_all(to_blocks(queries), "spatial", split_axis=0, concat_axis=0, tiled=True),
        lax.all_to_all(to_blocks(keys), "spatial", split_axis=0, concat_axis=0, tiled=True),
        lax.all_to_all(to_blocks(values), "spatial", split_axis=0, concat_axis=0, tiled=True),
    )
    add_key_block = from_blocks(key_block)
    add_value_block = from_blocks(value_block)
    paired = jnp.stack([add_key_block, add_value_block]).reshape(
        2, 1, TILE_T, height, split, TILE_W, part_channels
    )
    padded = with_halo(paired, (("temporal", 1), ("spatial", 4)), 1)
    query_block = from_blocks(query_block)
    column_base = lax.axis_index("spatial")
    offsets = jnp.arange(3, dtype=jnp.int32) - 1
    time_index = lax.axis_index("temporal") + offsets
    time_ok = (time_index >= 0) & (time_index < time_count)
    window_rows = min(3, tile_rows)
    heads_here = part_channels // D_HEAD
    width_index = column_base + 0 + offsets
    width_ok = (width_index >= 0) & (width_index < space_count)
    pattern_column = lax.dynamic_index_in_dim(window, 0, 2, keepdims=False)
    pattern_rows = pattern_column.reshape(tile_rows, 3, 3, 3)
    first_row = min(max(0 - 1, 0), tile_rows - window_rows)
    key_ok = tile_mask(pattern_rows[0], 0, first_row, window_rows, time_ok, width_ok)
    query_tile = query_block.reshape(-1, heads_here, D_HEAD)
    row_low = first_row * TILE_H
    row_high = row_low + window_rows * TILE_H
    key_window = padded[0, :, :, row_low:row_high, 0:3].reshape(-1, heads_here, D_HEAD)
    value_window = padded[1, :, :, row_low:row_high, 0:3].reshape(-1, heads_here, D_HEAD)
    attended_tile = attend(query_tile, key_window, value_window, key_ok)
    outputs = attended_tile.reshape(TILE_T, TILE_H, TILE_W, part_channels)
    result = outputs.reshape(space_count, shard_rows, span, part_channels)
    returned = lax.all_to_all(result, "spatial", split_axis=0, concat_axis=0, tiled=True)
    shaped = returned.reshape(split, groups, shard_rows, span, part_channels)
    return jnp.transpose(shaped, (2, 1, 3, 0, 4)).reshape(tokens_dev, channels)


def flipped(index, bits):
    bit = 1
    while bit <= bits:
        if bits & bit:
            index = index + bit - 2 * bit * ((index // bit) % 2)
        bit *= 2
    return index


def by_tiles(rows, count):
    width = count * TILE_W
    whole = rows.astype(jnp.float32)
    lines = whole.shape[0] // width
    return [
        jnp.concatenate(
            [whole[r * width + w * TILE_W : r * width + (w + 1) * TILE_W] for r in range(lines)],
            axis=0,
        ).astype(rows.dtype)
        for w in range(count)
    ]


def by_rows(parts):
    parts = [part.astype(jnp.float32) for part in parts]
    lines = parts[0].shape[0] // TILE_W
    return jnp.concatenate(
        [part[r * TILE_W : (r + 1) * TILE_W] for r in range(lines) for part in parts], axis=0
    ).astype(jnp.bfloat16)


def column_groups(count):
    first = min(2, count)
    return [(0, first)] + [(c, 1) for c in range(first, count)]


def fused_kernel(
    times, count, own_heads,
    q_hbm, k_hbm, v_hbm, win_hbm, out_ref,
    q_ref, k_ref, v_ref, win_ref, stage_kv, stage_q, kv, qs, outs, arrived, win,
    kv_send, kv_recv, q_send, q_recv, z_send, z_recv, o_send, o_recv, w_send, w_recv,
    in_sem, win_sem,
):
    t = lax.axis_index("temporal")
    me = lax.axis_index("spatial")
    part = q_ref.shape[0] // count
    peers = range(1, count)
    peer = [flipped(me, d) for d in range(count)]

    def rows_of(index):
        return pl.ds(pl.multiple_of(index * part, part), part)

    def columns_of(index, h):
        return pl.ds(pl.multiple_of((index * own_heads + h) * D_HEAD, D_HEAD), D_HEAD)

    def to(d):
        return {"spatial": peer[d]}

    def kv_copy(d, h, shard):
        return pltpu.make_async_remote_copy(
            src_ref=stage_kv.at[d - 1, h],
            dst_ref=kv.at[1, h, shard],
            send_sem=kv_send.at[d - 1, h],
            recv_sem=kv_recv.at[d - 1, h],
            device_id=to(d), device_id_type=MESH,
        )

    def q_copy(d, h, shard):
        return pltpu.make_async_remote_copy(
            src_ref=stage_q.at[d - 1, h],
            dst_ref=qs.at[h, shard],
            send_sem=q_send.at[d - 1, h],
            recv_sem=q_recv.at[d - 1, h],
            device_id=to(d), device_id_type=MESH,
        )

    def w_copy(d, slot):
        return pltpu.make_async_remote_copy(
            src_ref=win.at[slot],
            dst_ref=win.at[slot],
            send_sem=w_send.at[d - 1],
            recv_sem=w_recv.at[d - 1],
            device_id=to(d), device_id_type=MESH,
        )

    def groups(h):
        return column_groups(count) if h + 1 == own_heads else [(0, count)]

    def z_copy(side, d, h, j):
        tiles = pl.ds(*groups(h)[j])
        return pltpu.make_async_remote_copy(
            src_ref=kv.at[1, h, peer[d], :, tiles],
            dst_ref=kv.at[2 * side, h, peer[d], :, tiles],
            send_sem=z_send.at[side, d, h, j],
            recv_sem=z_recv.at[side, d, h, j],
            device_id={"temporal": t + 1 - 2 * side}, device_id_type=MESH,
        )

    def o_copy(d, h, w):
        return pltpu.make_async_remote_copy(
            src_ref=outs.at[h, w, rows_of(peer[d])],
            dst_ref=arrived.at[d - 1, h, w],
            send_sem=o_send.at[d - 1, h, w],
            recv_sem=o_recv.at[d - 1, h, w],
            device_id=to(d), device_id_type=MESH,
        )

    def in_copy(i, d, h):
        here = columns_of(peer[d], h)
        return pltpu.make_async_copy(
            (k_hbm, v_hbm, q_hbm)[i].at[:, here],
            (k_ref, v_ref, q_ref)[i].at[:, here],
            in_sem.at[i, d, h],
        )

    for h in range(own_heads):
        for d in range(count):
            for i in range(2):
                in_copy(i, d, h).start()
    win_copy = pltpu.make_async_copy(win_hbm, win_ref, win_sem)
    win_copy.start()
    for h in range(own_heads):
        for d in range(count):
            in_copy(2, d, h).start()

    can_send = (t < times - 1, t > 0)
    can_take = (t > 0, t < times - 1)

    barrier = pltpu.get_barrier_semaphore()
    for d in peers:
        pl.semaphore_signal(barrier, inc=1, device_id=to(d), device_id_type=MESH)
    for side in range(2):
        @pl.when(can_send[side])
        def _(side=side):
            pl.semaphore_signal(
                barrier, inc=1, device_id={"temporal": t + 1 - 2 * side}, device_id_type=MESH
            )

    def lay_kv(d, h):
        for i, ref in enumerate((k_ref, v_ref)):
            in_copy(i, d, h).wait()
            for w, piece in enumerate(by_tiles(ref[:, columns_of(peer[d], h)], count)):
                if d:
                    stage_kv[d - 1, h, i, w] = piece
                else:
                    kv[1, h, me, i, w] = piece

    def lay_q(d, h):
        in_copy(2, d, h).wait()
        for w, piece in enumerate(by_tiles(q_ref[:, columns_of(peer[d], h)], count)):
            if d:
                stage_q[d - 1, h, w] = piece
            else:
                qs[h, me, w] = piece

    def forward(d, h, some=slice(None)):
        for side in range(2):
            @pl.when(can_send[side])
            def _(side=side):
                for j in range(len(groups(h)))[some]:
                    z_copy(side, d, h, j).start()

    def forward_late(h, some):
        for d in range(count):
            if h < own_heads and not early(d, h):
                forward(d, h, some)

    def take(h, some=slice(None)):
        for side in range(2):
            @pl.when(can_take[side])
            def _(side=side):
                for j in range(len(groups(h)))[some]:
                    for d in range(count):
                        z_copy(side, d, h, j).wait_recv()

    lay_kv(0, 0)
    win_copy.wait()
    win[me] = jnp.zeros(win.shape[1:], win.dtype)
    win[me, 0:1, 0 : win_ref.shape[1]] = win_ref[...]
    for side in range(2):
        @pl.when(jnp.logical_not(can_take[side]))
        def _(side=side):
            kv[2 * side] = jnp.zeros(kv.shape[1:], kv.dtype)

    linked = can_send[0].astype(jnp.int32) + can_send[1].astype(jnp.int32)
    pl.semaphore_wait(barrier, count - 1 + linked)

    def early(d, h):
        return h == 0 or (h == 1 and d <= 1)

    forward(0, 0)
    for d in peers:
        lay_kv(d, 0)
        kv_copy(d, 0, me).start()
    for d in peers:
        w_copy(d, me).start()
    for h in range(1, own_heads):
        for d in range(count):
            lay_kv(d, h)
            if d == 0 and early(d, h):
                forward(d, h)
    for h in range(own_heads):
        for d in range(count):
            lay_q(d, h)

    for h in range(own_heads):
        for d in peers:
            kv_copy(d, h, peer[d]).wait_recv()
            if early(d, h):
                forward(d, h)
            if h + 1 < own_heads:
                kv_copy(d, h + 1, me).start()
            else:
                q_copy(d, 0, me).start()
    for d in peers:
        w_copy(d, peer[d]).wait_recv()

    def bring_home(h):
        out_ref[:, columns_of(me, h)] = by_rows([outs[h, w, rows_of(me)] for w in range(count)])
        for d in peers:
            for w in range(count):
                o_copy(d, h, w).wait_recv()
            out_ref[:, columns_of(peer[d], h)] = by_rows([arrived[d - 1, h, w] for w in range(count)])

    def window_of(h, i, low, high):
        return jnp.concatenate(
            [kv[p, h, f, i, c] for p in range(3) for c in range(low, high) for f in range(count)],
            axis=0,
        )

    factor = math.log2(math.e) / math.sqrt(D_HEAD)
    for h in range(own_heads):
        for d in peers:
            q_copy(d, h, peer[d]).wait_recv()
            if h + 1 < own_heads:
                q_copy(d, h + 1, me).start()
        last = h + 1 == own_heads
        if not last:
            take(h)
            forward_late(h + 1, slice(0, 2))
        for w in range(count):
            if last and w < len(groups(h)):
                if w + 1 == len(groups(h)) and h:
                    bring_home(h - 1)
                take(h, slice(w, w + 1))
            if not last and w == count // 2:
                forward_late(h + 1, slice(2, None))
            low, high = max(w - 1, 0), min(w + 2, count)
            query = qs[h, :, w].reshape(-1, D_HEAD)
            pattern = win[w, 0:1, :]
            wide = high - low
            keys = window_of(h, 0, low, high)
            scores = lax.dot_general(
                query, keys, (((1,), (1,)), ((), ())), preferred_element_type=jnp.float32
            )
            blocks, limits, peak = [], [], None
            for i in range(3 * wide):
                p, c = i // wide, low + i % wide
                start = i * query.shape[0]
                halves = [
                    scores[:, j : j + LANES] for j in range(start, start + query.shape[0], LANES)
                ]
                entry = 9 * p + 3 + (c - w + 1)
                ok = pattern[:, entry : entry + 1] == 1
                if p != 1:
                    ok = jnp.logical_and(ok, can_take[p // 2])
                limit = jnp.where(ok, 0.0, jnp.inf).astype(jnp.float32)
                top = functools.reduce(jnp.maximum, halves) - limit
                peak = top if peak is None else jnp.maximum(peak, top)
                blocks.append(halves)
                limits.append(limit)
            peak = jnp.broadcast_to(jnp.max(peak, axis=1, keepdims=True), peak.shape)
            total, rounded = None, []
            for halves, limit in zip(blocks, limits):
                base = peak + limit
                for half in halves:
                    weights = jnp.exp2((half - base) * factor)
                    total = weights if total is None else total + weights
                    rounded.append(weights.astype(jnp.bfloat16))
            total = jnp.sum(total, axis=1, keepdims=True)
            mixed = jnp.dot(
                jnp.concatenate(rounded, axis=1),
                window_of(h, 1, low, high),
                preferred_element_type=jnp.float32,
            )
            outs[h, w] = (mixed / total).astype(jnp.bfloat16)
            for d in peers:
                o_copy(d, h, w).start()

    bring_home(own_heads - 1)

    for h in range(own_heads):
        for d in peers:
            kv_copy(d, h, me).wait_send()
            q_copy(d, h, me).wait_send()
            for w in range(count):
                o_copy(d, h, w).wait_send()
        for side in range(2):
            @pl.when(can_send[side])
            def _(side=side):
                for d in range(count):
                    for j in range(len(groups(h))):
                        z_copy(side, d, h, j).wait_send()
    for d in peers:
        w_copy(d, me).wait_send()


def settle_kernel(source, result, sems):
    parts = sems.shape[0]
    rows = source.shape[0] // parts
    copies = [
        pltpu.make_async_copy(
            source.at[pl.ds(i * rows, rows)], result.at[pl.ds(i * rows, rows)], sems.at[i]
        )
        for i in range(parts)
    ]
    for copy in copies:
        copy.start()
    for copy in copies:
        copy.wait()


def settle(array):
    return pl.pallas_call(
        settle_kernel,
        out_shape=jax.ShapeDtypeStruct(array.shape, array.dtype),
        in_specs=[pl.BlockSpec(memory_space=pl.ANY)],
        out_specs=pl.BlockSpec(memory_space=pl.ANY),
        scratch_shapes=[pltpu.SemaphoreType.DMA((8,))],
        compiler_params=pltpu.CompilerParams(vmem_limit_bytes=60 * 2**20),
    )(array)


def fused(queries, keys, values, window):
    count, times = lax.axis_size("spatial"), lax.axis_size("temporal")
    tokens, channels = queries.shape
    own = channels // (D_HEAD * count)
    part = tokens // count
    groups = len(column_groups(count))
    vmem = pl.BlockSpec(memory_space=pltpu.VMEM)
    dma = pltpu.SemaphoreType.DMA
    pairs = own * count * (3 * count - 2) * 3 * tokens * tokens * D_HEAD
    return pl.pallas_call(
        functools.partial(fused_kernel, times, count, own),
        out_shape=jax.ShapeDtypeStruct(queries.shape, queries.dtype),
        in_specs=[pl.BlockSpec(memory_space=pl.ANY)] * 4,
        out_specs=vmem,
        scratch_shapes=[
            pltpu.VMEM(queries.shape, jnp.bfloat16),
            pltpu.VMEM(queries.shape, jnp.bfloat16),
            pltpu.VMEM(queries.shape, jnp.bfloat16),
            pltpu.VMEM((1, window.size), jnp.int32),
            pltpu.VMEM((count - 1, own, 2, count, part, D_HEAD), jnp.bfloat16),
            pltpu.VMEM((count - 1, own, count, part, D_HEAD), jnp.bfloat16),
            pltpu.VMEM((3, own, count, 2, count, part, D_HEAD), jnp.bfloat16),
            pltpu.VMEM((own, count, count, part, D_HEAD), jnp.bfloat16),
            pltpu.VMEM((own, count, tokens, D_HEAD), jnp.bfloat16),
            pltpu.VMEM((count - 1, own, count, part, D_HEAD), jnp.bfloat16),
            pltpu.VMEM((count, 8, 128), jnp.int32),
            dma((count - 1, own)), dma((count - 1, own)),
            dma((count - 1, own)), dma((count - 1, own)),
            dma((2, count, own, groups)), dma((2, count, own, groups)),
            dma((count - 1, own, count)), dma((count - 1, own, count)),
            dma((count - 1,)), dma((count - 1,)),
            dma((3, count, own)), dma,
        ],
        compiler_params=pltpu.CompilerParams(
            collective_id=0, has_side_effects=True, vmem_limit_bytes=60 * 2**20
        ),
        cost_estimate=pl.CostEstimate(
            flops=4 * pairs, bytes_accessed=4 * tokens * channels * 2, transcendentals=pairs // D_HEAD
        ),
    )(queries, keys, values, window.reshape(1, -1))


def body(queries, keys, values, window):
    count = lax.axis_size("spatial")
    tokens, channels = queries.shape
    heads_here = channels // D_HEAD
    whole_tiles = window.shape[1] == 1 and window.shape[2] == 1 and tokens == TILE_T * TILE_H * TILE_W
    if whole_tiles and count & (count - 1) == 0 and heads_here % count == 0:
        return settle(fused(queries, keys, values, window))
    return gathered(queries, keys, values, window)


def solution(mesh):
    return jax.shard_map(
        body,
        mesh=mesh,
        in_specs=(
            P(("temporal", "spatial"), "head"),
            P(("temporal", "spatial"), "head"),
            P(("temporal", "spatial"), "head"),
            P("temporal", None, "spatial", None),
        ),
        out_specs=P(("temporal", "spatial"), "head"),
        check_vma=False,
    )
```
